256 devices in a mesh: bl: 8 (over z), lst: 32 (over y, x, core).
Axes of the slice: x: 4, y: 4, z: 8, core: 2. Of those that a mesh axis runs over, the one named last changes fastest.
Arguments:
- visibility: bfloat16 [4, 1024, 32, 3072], P(None, 'lst', 'bl'), may hold values from -6 to 6
- start_bin: int32 [4], replicated, may hold values from 0 to 1023
- coverage: int32 [4], replicated, may hold values from 256 to 1024
- clip_flags: int32 [4, 1024, 32], P(None, 'lst', 'bl'), may hold values 0 or 1
- fringe_filter: bfloat16 [1024, 1024], P('bl'), may hold values from -0.1875 to 0.1875
Outputs:
- filtered: bfloat16 [1024, 32, 3072], P('lst', 'bl')
- spread: bfloat16 [1024, 32, 3072], P('lst', 'bl')
The draws below stay inside these ranges and needn't reach their ends.
All inputs are finite; a program needn't handle non-finite values. No bound on the sum of `clip_flags` on one device may be relied on, other than what follows from the above.
Results may differ from the reference program's by a relative error of at most 0.0047.
Values may be sent and summed in bfloat16 or wider, within the bound.
A program may use at most 128 MiB of HBM per device.

```python
import jax
import jax.numpy as jnp
from jax import lax

CH = 1536
LSTBINS = 1024
NIGHTS = 4
BL = 32


def plant(result, own_key, least, high):
    place = [jax.random.randint(jax.random.fold_in(own_key, axis), (), 0, length) for axis, length in enumerate(result.shape)]
    widest = result.shape.index(max(result.shape))
    beside = place[:widest] + [(place[widest] + 1) % result.shape[widest]] + place[widest + 1:]
    return result.at[tuple(place)].set(least).at[tuple(beside)].set(high)


def level_of(rng, extent, shards, least, high):
    level, own = 1.0, jax.random.fold_in(rng, 6)
    for axis_at, blocks in shards:
        steps = jnp.exp(jax.random.uniform(jax.random.fold_in(own, axis_at), (blocks,), jnp.float32, least / len(shards), high / len(shards)))
        level = level * jnp.repeat(steps, extent[axis_at] // blocks).reshape([-1 if axis == axis_at else 1 for axis in range(len(extent))])
    return level


def centred(key, extent, scale, reach, cuts=(), held_as=jnp.bfloat16):
    result = jax.random.normal(key, extent, jnp.float32) * scale
    if len(cuts) > 0:
        result = level_of(key, extent, cuts, -0.22, 0.18) * result
    return jnp.clip(result, min=-reach, max=reach).astype(held_as)


def setup_inputs(seed: int = 0) -> dict:
    streams_of = jax.random.split(jax.random.key(seed), 6)
    return {
        "visibility": centred(streams_of[0], (NIGHTS, LSTBINS, BL, 2 * CH), 1.0, 6.0, ((1, 32), (2, 8))),
        "start_bin": plant(jax.random.randint(streams_of[1], (NIGHTS,), 0, LSTBINS), jax.random.fold_in(streams_of[1], 1), 0, LSTBINS - 1).astype(jnp.int32),
        "coverage": plant(jax.random.randint(streams_of[2], (NIGHTS,), LSTBINS // 4, LSTBINS + 1), jax.random.fold_in(streams_of[2], 1), LSTBINS // 4, LSTBINS).astype(jnp.int32),
        "clip_flags": plant((jax.random.randint(streams_of[3], (NIGHTS, LSTBINS, BL), 0, 8) < 1).astype(jnp.int32), jax.random.fold_in(streams_of[3], 1), 0, 1),
        "fringe_filter": centred(streams_of[4], (LSTBINS, LSTBINS), LSTBINS ** -0.5, 0.1875, ((0, 8),)),
    }


def rotate_bins(series, first_bin):
    doubled = jnp.concatenate([series, series], axis=0)
    start_row = ((LSTBINS - first_bin) % LSTBINS).astype(jnp.int32)
    return lax.dynamic_slice_in_dim(doubled, start_row, LSTBINS, 0)


def reference(visibility, start_bin, coverage, clip_flags, fringe_filter):
    integration = jnp.arange(LSTBINS, dtype=jnp.int32)
    present_mask = integration[None, :] < coverage[:, None]
    usable = jnp.logical_and(present_mask[:, :, None], clip_flags == 0).astype(jnp.float32)
    filter_wide = fringe_filter.astype(jnp.float32)

    def per_baseline(baseline):
        samples = lax.dynamic_index_in_dim(visibility, baseline, 2, keepdims=False).astype(jnp.float32)
        weight = lax.dynamic_index_in_dim(usable, baseline, 2, keepdims=False)
        aligned = jax.vmap(rotate_bins)(samples, start_bin)
        weight = jax.vmap(rotate_bins)(weight, start_bin)[:, :, None]
        weight_sum = jnp.sum(weight, axis=0)
        average = jnp.sum(weight * aligned, axis=0) / jnp.maximum(weight_sum, 1.0)
        spread = jnp.sum(weight * (aligned - average) ** 2, axis=0) / jnp.maximum(weight_sum - 1.0, 1.0)
        rounded = lax.optimization_barrier(average.astype(jnp.bfloat16)).astype(jnp.float32)
        filtered = jnp.dot(filter_wide, rounded, precision=lax.Precision.HIGHEST)
        return filtered.astype(jnp.bfloat16), spread.astype(jnp.bfloat16)

    filtered, spread = lax.map(per_baseline, jnp.arange(BL, dtype=jnp.int32))
    return jnp.transpose(filtered, (1, 0, 2)), jnp.transpose(spread, (1, 0, 2))
```

```python
import functools

import jax
import jax.numpy as jnp
from jax import lax
from jax.experimental import pallas as pl
from jax.experimental.pallas import tpu as pltpu
from jax.sharding import PartitionSpec as P

LANES = 128


def total_wait(ref, sem):
    pltpu.make_async_copy(ref, ref, sem).wait()


def kernel(
    sizes,
    start_ref,
    cover_ref,
    flags_ref,
    vis_hbm,
    filt_hbm,
    out_f,
    out_s,
    vis,
    stage,
    send_in,
    recv_in,
    w_send,
    w_recv,
    rows,
    w_rows,
    w_al,
    inv_mean,
    inv_var,
    filt,
    means,
    send_out,
    recv_out,
    vis_sem,
    in_send,
    in_recv,
    w_sems,
    f_send,
    f_recv,
    out_send,
    out_recv,
):
    nights, block, bls, lst_n, bl_n, tiles = sizes
    groups = lst_n // bls
    bins = block * lst_n
    me = lax.axis_index("lst")
    zed = lax.axis_index("bl")
    core = lax.rem(me, 2)
    partner = me + 1 - 2 * core
    my_b, my_g = me // groups, lax.rem(me, groups)
    half = filt.shape[2]

    barrier = pltpu.get_barrier_semaphore()

    def greet_lst(i, _):
        pl.semaphore_signal(barrier, 1, device_id={"lst": lax.rem(me + i, lst_n)})
        return 0

    def greet_bl(i, _):
        pl.semaphore_signal(barrier, 1, device_id={"bl": lax.rem(zed + i, bl_n)})
        return 0

    load = pltpu.make_async_copy(vis_hbm, vis, vis_sem)
    load.start()
    lax.fori_loop(1, lst_n, greet_lst, 0)
    lax.fori_loop(1, bl_n, greet_bl, 0)

    own_half = pltpu.make_async_copy(
        filt_hbm.at[pl.ds(pl.multiple_of(core * half, half), half)],
        filt.at[zed, core],
        f_recv.at[0],
    )
    own_half.start()

    lane = lax.broadcasted_iota(jnp.int32, (1, block), 1) + me * block
    w_send[...] = jnp.zeros_like(w_send)
    for n in range(nights):
        seen = lane < cover_ref[n]
        for b in range(bls):
            good = jnp.logical_and(seen, flags_ref[n, b : b + 1, :] == 0)
            w_send[b, n : n + 1, 0:block] = jnp.where(good, 1.0, 0.0).astype(jnp.float32)

    load.wait()

    def regroup(tile, group):
        lanes = pl.ds(pl.multiple_of((group * tiles + tile) * LANES, LANES), LANES)
        for n in range(nights):
            for t in range(block):
                stage[n, t * bls : (t + 1) * bls, :] = vis[n, t, :, lanes].astype(jnp.float32)
            for b in range(bls):
                piece = stage[n, pl.ds(b, block, stride=bls), :]
                send_in[tile, b * groups + group, n] = piece.astype(jnp.bfloat16)

    def order(step):
        far = (step + 1) // 2
        return lax.rem(my_g + jnp.where(lax.rem(step, 2) == 1, far, groups - far), groups)

    def send_group(tile, group):
        for i in (1, 3, 2, 0):
            b = lax.rem(my_b + i, bls)
            q = b * groups + group

            def remote():
                pltpu.make_async_remote_copy(
                    send_in.at[tile, q],
                    recv_in.at[tile, me],
                    in_send.at[tile],
                    in_recv.at[tile],
                    device_id={"lst": q},
                ).start()

            if i == 0:
                pl.when(group != my_g)(remote)

                @pl.when(group == my_g)
                def _():
                    pltpu.make_async_copy(
                        send_in.at[tile, q], recv_in.at[tile, me], in_recv.at[tile]
                    ).start()
            else:
                remote()

    regroup(0, order(0))
    pl.semaphore_wait(barrier, lst_n - 1 + bl_n - 1)
    send_group(0, order(0))

    def send_half(i, _):
        pltpu.make_async_remote_copy(
            filt_hbm.at[pl.ds(pl.multiple_of(core * half, half), half)],
            filt.at[zed, core],
            f_send.at[0],
            f_recv.at[0],
            device_id={"bl": lax.rem(zed + i, bl_n)},
        ).start()
        return 0

    lax.fori_loop(1, bl_n, send_half, 0)

    def send_weights(i, _):
        q = lax.rem(me + i, lst_n)
        pltpu.make_async_remote_copy(
            w_send.at[q // groups], w_recv.at[me], w_sems.at[0], w_sems.at[1], device_id={"lst": q}
        ).start()
        return 0

    lax.fori_loop(1, lst_n, send_weights, 0)
    pltpu.make_async_copy(w_send.at[my_b], w_recv.at[me], w_sems.at[1]).start()

    def send_step(step, _):
        tile = step // groups
        group = order(lax.rem(step, groups))
        regroup(tile, group)
        send_group(tile, group)
        return 0

    lax.fori_loop(1, tiles * groups, send_step, 0)

    total_wait(w_recv, w_sems.at[1])
    shape = (block, LANES)
    diagonal = lax.broadcasted_iota(jnp.int32, shape, 0) == lax.broadcasted_iota(
        jnp.int32, shape, 1
    )

    def spread_weights(src, _):
        for n in range(nights):
            row = jnp.broadcast_to(w_recv[src, n : n + 1, :], shape)
            column = jnp.sum(jnp.where(diagonal, row, 0.0), axis=1, keepdims=True)
            at = pl.ds(pl.multiple_of(src * block, block), block)
            w_rows[n, at, :] = jnp.broadcast_to(column, shape)
        return 0

    lax.fori_loop(0, lst_n, spread_weights, 0)
    for n in range(nights):
        w_rows[n, bins : bins + block, :] = w_rows[n, 0:block, :]

    def first_row(n, k):
        return lax.rem(k * block + bins - start_ref[n], bins)

    def align_weights(k, _):
        at = pl.ds(pl.multiple_of(k * block, block), block)
        count = jnp.zeros(shape, jnp.float32)
        for n in range(nights):
            w = w_rows[n, pl.ds(first_row(n, k), block), :]
            w_al[n, at, :] = w
            count = count + w
        inv_mean[at, :] = 1.0 / jnp.maximum(count, 1.0)
        inv_var[at, :] = 1.0 / jnp.maximum(count - 1.0, 1.0)
        return 0

    lax.fori_loop(0, lst_n, align_weights, 0)

    total_wait(filt.at[:, core], f_recv.at[0])
    swap = pltpu.make_async_remote_copy(
        filt.at[:, core],
        filt.at[:, core],
        f_send.at[1],
        f_recv.at[1],
        device_id={"lst": partner},
    )
    swap.start()

    def bin_tile(tile, _):
        total_wait(recv_in.at[tile], in_recv.at[tile])

        def widen(src, _):
            at = pl.ds(pl.multiple_of(src * block, block), block)
            for n in range(nights):
                rows[n, at, :] = recv_in[tile, src, n].astype(jnp.float32)
            return 0

        lax.fori_loop(0, lst_n, widen, 0)
        for n in range(nights):
            rows[n, bins : bins + block, :] = rows[n, 0:block, :]

        def moments(k, _):
            at = pl.ds(pl.multiple_of(k * block, block), block)
            x = [rows[n, pl.ds(first_row(n, k), block), :] for n in range(nights)]
            w = [w_al[n, at, :] for n in range(nights)]
            total = x[0] * w[0]
            for n in range(1, nights):
                total = total + x[n] * w[n]
            mean = total * inv_mean[at, :]
            square = jnp.zeros(shape, jnp.float32)
            for n in range(nights):
                off = x[n] - mean
                square = square + w[n] * (off * off)
            means[at, :] = mean.astype(jnp.bfloat16)
            send_out[tile, k, 1] = (square * inv_var[at, :]).astype(jnp.bfloat16)
            return 0

        lax.fori_loop(0, lst_n, moments, 0)

        @pl.when(tile == 0)
        def _():
            total_wait(filt.at[:, 1 - core], f_recv.at[1])

        def apply_filter(z, _):
            product = jnp.dot(
                filt[z].reshape(2 * half, bins), means[...], preferred_element_type=jnp.float32
            ).astype(jnp.bfloat16)
            per = 2 * half // block
            for r in range(per):
                send_out[tile, z * per + r, 0] = product[r * block : (r + 1) * block, :]
            return 0

        lax.fori_loop(0, bl_n, apply_filter, 0)

        def send_back(i, _):
            q = lax.rem(me + i, lst_n)
            pltpu.make_async_remote_copy(
                send_out.at[tile, q],
                recv_out.at[tile, me],
                out_send.at[tile],
                out_recv.at[tile],
                device_id={"lst": q},
            ).start()
            return 0

        lax.fori_loop(1, lst_n, send_back, 0)
        pltpu.make_async_copy(
            send_out.at[tile, me], recv_out.at[tile, me], out_recv.at[tile]
        ).start()
        return 0

    lax.fori_loop(0, tiles, bin_tile, 0)

    def place_tile(tile, _):
        total_wait(recv_out.at[tile], out_recv.at[tile])

        def place(group, _):
            lanes = pl.ds(pl.multiple_of((group * tiles + tile) * LANES, LANES), LANES)
            for which, out in ((0, out_f), (1, out_s)):
                for b in range(bls):
                    stage[which, pl.ds(b, block, stride=bls), :] = recv_out[
                        tile, b * groups + group, which
                    ].astype(jnp.float32)
                for t in range(block):
                    out[t, :, lanes] = stage[which, t * bls : (t + 1) * bls, :].astype(
                        jnp.bfloat16
                    )
            return 0

        lax.fori_loop(0, groups, place, 0)
        return 0

    lax.fori_loop(0, tiles, place_tile, 0)

    for tile in range(tiles):
        total_wait(send_in.at[tile, pl.ds(0, lst_n - 1)], in_send.at[tile])
        total_wait(send_out.at[tile, pl.ds(0, lst_n - 1)], out_send.at[tile])
    total_wait(w_recv.at[pl.ds(0, lst_n - 1)], w_sems.at[0])
    total_wait(filt.at[pl.ds(0, bl_n - 1), 0], f_send.at[0])
    total_wait(filt.at[:, 0], f_send.at[1])


def shards(visibility, start_bin, coverage, clip_flags, fringe_filter):
    lst_n, bl_n = lax.axis_size("lst"), lax.axis_size("bl")
    nights, block, bls, width = visibility.shape
    rows, bins = fringe_filter.shape
    groups = lst_n // bls
    tiles = width // (groups * LANES)
    sizes = (nights, block, bls, lst_n, bl_n, tiles)
    bf16, f32 = jnp.bfloat16, jnp.float32
    out = jax.ShapeDtypeStruct((block, bls, width), bf16)
    smem = pl.BlockSpec(memory_space=pltpu.SMEM)
    vmem = pl.BlockSpec(memory_space=pltpu.VMEM)
    hbm = pl.BlockSpec(memory_space=pl.ANY)
    dma = pltpu.SemaphoreType.DMA
    return pl.pallas_call(
        functools.partial(kernel, sizes),
        out_shape=(out, out),
        in_specs=[smem, smem, vmem, hbm, hbm],
        out_specs=(vmem, vmem),
        scratch_shapes=[
            pltpu.VMEM(visibility.shape, bf16),
            pltpu.VMEM((nights, block * bls, LANES), f32),
            pltpu.VMEM((tiles, lst_n, nights, block, LANES), bf16),
            pltpu.VMEM((tiles, lst_n, nights, block, LANES), bf16),
            pltpu.VMEM((bls, nights, LANES), f32),
            pltpu.VMEM((lst_n, nights, LANES), f32),
            pltpu.VMEM((nights, bins + block, LANES), f32),
            pltpu.VMEM((nights, bins + block, LANES), f32),
            pltpu.VMEM((nights, bins, LANES), f32),
            pltpu.VMEM((bins, LANES), f32),
            pltpu.VMEM((bins, LANES), f32),
            pltpu.VMEM((bl_n, 2, rows // 2, bins), bf16),
            pltpu.VMEM((bins, LANES), bf16),
            pltpu.VMEM((tiles, lst_n, 2, block, LANES), bf16),
            pltpu.VMEM((tiles, lst_n, 2, block, LANES), bf16),
            dma,
            dma((tiles,)),
            dma((tiles,)),
            dma((2,)),
            dma((2,)),
            dma((2,)),
            dma((tiles,)),
            dma((tiles,)),
        ],
        compiler_params=pltpu.CompilerParams(
            collective_id=0, has_side_effects=True, vmem_limit_bytes=48 * 2**20
        ),
        cost_estimate=pl.CostEstimate(
            flops=2 * bins * bins * tiles * LANES, bytes_accessed=8 * 2**20, transcendentals=0
        ),
    )(start_bin, coverage, jnp.swapaxes(clip_flags, 1, 2), visibility, fringe_filter)


def solution(mesh):
    placed = (P(None, "lst", "bl", None), P(), P(), P(None, "lst", "bl"), P("bl", None))
    return jax.shard_map(
        shards,
        mesh=mesh,
        in_specs=placed,
        out_specs=(P("lst", "bl", None), P("lst", "bl", None)),
        check_vma=False,
    )
```

```python
import functools

import jax
import jax.numpy as jnp
from jax import lax
from jax.experimental import pallas as pl
from jax.experimental.pallas import tpu as pltpu
from jax.sharding import PartitionSpec as P

LANES = 128


def total_wait(ref, sem):
    pltpu.make_async_copy(ref, ref, sem).wait()


def kernel(
    sizes,
    start_hbm,
    cover_hbm,
    flags_hbm,
    vis_hbm,
    filt_hbm,
    out_f,
    out_s,
    start_ref,
    cover_ref,
    flags_ref,
    vis,
    stage,
    send_in,
    recv_in,
    w_send,
    w_recv,
    rows,
    w_rows,
    w_al,
    inv_mean,
    inv_var,
    filt,
    means,
    send_out,
    recv_out,
    vis_sem,
    small_sems,
    in_send,
    in_recv,
    w_sems,
    f_send,
    f_recv,
    out_send,
    out_recv,
):
    nights, block, bls, lst_n, bl_n, tiles = sizes
    groups = lst_n // bls
    bins = block * lst_n
    me = lax.axis_index("lst")
    zed = lax.axis_index("bl")
    core = lax.rem(me, 2)
    partner = me + 1 - 2 * core
    my_b, my_g = me // groups, lax.rem(me, groups)
    half = filt.shape[2]

    barrier = pltpu.get_barrier_semaphore()

    def greet_lst(i, _):
        pl.semaphore_signal(barrier, 1, device_id={"lst": lax.rem(me + i, lst_n)})
        return 0

    def greet_bl(i, _):
        pl.semaphore_signal(barrier, 1, device_id={"bl": lax.rem(zed + i, bl_n)})
        return 0

    load = pltpu.make_async_copy(vis_hbm, vis, vis_sem)
    small = [
        pltpu.make_async_copy(src, dst, small_sems.at[i])
        for i, (src, dst) in enumerate(
            ((start_hbm, start_ref), (cover_hbm, cover_ref), (flags_hbm, flags_ref))
        )
    ]
    for copy in small:
        copy.start()
    load.start()
    lax.fori_loop(1, lst_n, greet_lst, 0)
    lax.fori_loop(1, bl_n, greet_bl, 0)

    own_half = pltpu.make_async_copy(
        filt_hbm.at[pl.ds(pl.multiple_of(core * half, half), half)],
        filt.at[zed, core],
        f_recv.at[0],
    )
    own_half.start()

    for copy in small:
        copy.wait()

    lane = lax.broadcasted_iota(jnp.int32, (1, block), 1) + me * block
    w_send[...] = jnp.zeros_like(w_send)
    for n in range(nights):
        seen = lane < cover_ref[n]
        for b in range(bls):
            good = jnp.logical_and(seen, flags_ref[n, b : b + 1, :] == 0)
            w_send[b, n : n + 1, 0:block] = jnp.where(good, 1.0, 0.0).astype(jnp.float32)

    load.wait()

    def regroup(tile, group):
        lanes = pl.ds(pl.multiple_of((group * tiles + tile) * LANES, LANES), LANES)
        for n in range(nights):
            for t in range(block):
                stage[n, t * bls : (t + 1) * bls, :] = vis[n, t, :, lanes].astype(jnp.float32)
            for b in range(bls):
                piece = stage[n, pl.ds(b, block, stride=bls), :]
                send_in[tile, b * groups + group, n] = piece.astype(jnp.bfloat16)

    def order(step):
        far = (step + 1) // 2
        return lax.rem(my_g + jnp.where(lax.rem(step, 2) == 1, far, groups - far), groups)

    def send_group(tile, group):
        for i in (1, 3, 2, 0):
            b = lax.rem(my_b + i, bls)
            q = b * groups + group

            def remote():
                pltpu.make_async_remote_copy(
                    send_in.at[tile, q],
                    recv_in.at[tile, me],
                    in_send.at[tile],
                    in_recv.at[tile],
                    device_id={"lst": q},
                ).start()

            if i == 0:
                pl.when(group != my_g)(remote)

                @pl.when(group == my_g)
                def _():
                    pltpu.make_async_copy(
                        send_in.at[tile, q], recv_in.at[tile, me], in_recv.at[tile]
                    ).start()
            else:
                remote()

    regroup(0, order(0))
    pl.semaphore_wait(barrier, lst_n - 1 + bl_n - 1)
    send_group(0, order(0))

    def send_half(i, _):
        pltpu.make_async_remote_copy(
            filt_hbm.at[pl.ds(pl.multiple_of(core * half, half), half)],
            filt.at[zed, core],
            f_send.at[0],
            f_recv.at[0],
            device_id={"bl": lax.rem(zed + i, bl_n)},
        ).start()
        return 0

    lax.fori_loop(1, bl_n, send_half, 0)

    def send_weights(i, _):
        q = lax.rem(me + i, lst_n)
        pltpu.make_async_remote_copy(
            w_send.at[q // groups], w_recv.at[me], w_sems.at[0], w_sems.at[1], device_id={"lst": q}
        ).start()
        return 0

    lax.fori_loop(1, lst_n, send_weights, 0)
    pltpu.make_async_copy(w_send.at[my_b], w_recv.at[me], w_sems.at[1]).start()

    def send_step(step, _):
        tile = step // groups
        group = order(lax.rem(step, groups))
        regroup(tile, group)
        send_group(tile, group)
        return 0

    lax.fori_loop(1, tiles * groups, send_step, 0)

    total_wait(w_recv, w_sems.at[1])
    shape = (block, LANES)
    diagonal = lax.broadcasted_iota(jnp.int32, shape, 0) == lax.broadcasted_iota(
        jnp.int32, shape, 1
    )

    def spread_weights(src, _):
        for n in range(nights):
            row = jnp.broadcast_to(w_recv[src, n : n + 1, :], shape)
            column = jnp.sum(jnp.where(diagonal, row, 0.0), axis=1, keepdims=True)
            at = pl.ds(pl.multiple_of(src * block, block), block)
            w_rows[n, at, :] = jnp.broadcast_to(column, shape)
        return 0

    lax.fori_loop(0, lst_n, spread_weights, 0)
    for n in range(nights):
        w_rows[n, bins : bins + block, :] = w_rows[n, 0:block, :]

    def first_row(n, k):
        return lax.rem(k * block + bins - start_ref[n], bins)

    def align_weights(k, _):
        at = pl.ds(pl.multiple_of(k * block, block), block)
        count = jnp.zeros(shape, jnp.float32)
        for n in range(nights):
            w = w_rows[n, pl.ds(first_row(n, k), block), :]
            w_al[n, at, :] = w
            count = count + w
        inv_mean[at, :] = 1.0 / jnp.maximum(count, 1.0)
        inv_var[at, :] = 1.0 / jnp.maximum(count - 1.0, 1.0)
        return 0

    lax.fori_loop(0, lst_n, align_weights, 0)

    total_wait(filt.at[:, core], f_recv.at[0])
    swap = pltpu.make_async_remote_copy(
        filt.at[:, core],
        filt.at[:, core],
        f_send.at[1],
        f_recv.at[1],
        device_id={"lst": partner},
    )
    swap.start()

    def bin_tile(tile, _):
        total_wait(recv_in.at[tile], in_recv.at[tile])

        def widen(src, _):
            at = pl.ds(pl.multiple_of(src * block, block), block)
            for n in range(nights):
                rows[n, at, :] = recv_in[tile, src, n].astype(jnp.float32)
            return 0

        lax.fori_loop(0, lst_n, widen, 0)
        for n in range(nights):
            rows[n, bins : bins + block, :] = rows[n, 0:block, :]

        def moments(k, _):
            at = pl.ds(pl.multiple_of(k * block, block), block)
            x = [rows[n, pl.ds(first_row(n, k), block), :] for n in range(nights)]
            w = [w_al[n, at, :] for n in range(nights)]
            total = x[0] * w[0]
            for n in range(1, nights):
                total = total + x[n] * w[n]
            mean = total * inv_mean[at, :]
            square = jnp.zeros(shape, jnp.float32)
            for n in range(nights):
                off = x[n] - mean
                square = square + w[n] * (off * off)
            means[at, :] = mean.astype(jnp.bfloat16)
            send_out[tile, k, 1] = (square * inv_var[at, :]).astype(jnp.bfloat16)
            return 0

        lax.fori_loop(0, lst_n, moments, 0)

        @pl.when(tile == 0)
        def _():
            total_wait(filt.at[:, 1 - core], f_recv.at[1])

        def apply_filter(z, _):
            product = jnp.dot(
                filt[z].reshape(2 * half, bins), means[...], preferred_element_type=jnp.float32
            ).astype(jnp.bfloat16)
            per = 2 * half // block
            for r in range(per):
                send_out[tile, z * per + r, 0] = product[r * block : (r + 1) * block, :]
            return 0

        lax.fori_loop(0, bl_n, apply_filter, 0)

        def send_back(i, _):
            q = lax.rem(me + i, lst_n)
            pltpu.make_async_remote_copy(
                send_out.at[tile, q],
                recv_out.at[tile, me],
                out_send.at[tile],
                out_recv.at[tile],
                device_id={"lst": q},
            ).start()
            return 0

        lax.fori_loop(1, lst_n, send_back, 0)
        pltpu.make_async_copy(
            send_out.at[tile, me], recv_out.at[tile, me], out_recv.at[tile]
        ).start()
        return 0

    lax.fori_loop(0, tiles, bin_tile, 0)

    def place_tile(tile, _):
        total_wait(recv_out.at[tile], out_recv.at[tile])

        def place(group, _):
            lanes = pl.ds(pl.multiple_of((group * tiles + tile) * LANES, LANES), LANES)
            for which, out in ((0, out_f), (1, out_s)):
                for b in range(bls):
                    stage[which, pl.ds(b, block, stride=bls), :] = recv_out[
                        tile, b * groups + group, which
                    ].astype(jnp.float32)
                for t in range(block):
                    out[t, :, lanes] = stage[which, t * bls : (t + 1) * bls, :].astype(
                        jnp.bfloat16
                    )
            return 0

        lax.fori_loop(0, groups, place, 0)
        return 0

    lax.fori_loop(0, tiles, place_tile, 0)

    for tile in range(tiles):
        total_wait(send_in.at[tile, pl.ds(0, lst_n - 1)], in_send.at[tile])
        total_wait(send_out.at[tile, pl.ds(0, lst_n - 1)], out_send.at[tile])
    total_wait(w_recv.at[pl.ds(0, lst_n - 1)], w_sems.at[0])
    total_wait(filt.at[pl.ds(0, bl_n - 1), 0], f_send.at[0])
    total_wait(filt.at[:, 0], f_send.at[1])


def shards(visibility, start_bin, coverage, clip_flags, fringe_filter):
    lst_n, bl_n = lax.axis_size("lst"), lax.axis_size("bl")
    nights, block, bls, width = visibility.shape
    rows, bins = fringe_filter.shape
    groups = lst_n // bls
    tiles = width // (groups * LANES)
    sizes = (nights, block, bls, lst_n, bl_n, tiles)
    bf16, f32 = jnp.bfloat16, jnp.float32
    out = jax.ShapeDtypeStruct((block, bls, width), bf16)
    vmem = pl.BlockSpec(memory_space=pltpu.VMEM)
    hbm = pl.BlockSpec(memory_space=pltpu.HBM)
    dma = pltpu.SemaphoreType.DMA
    return pl.pallas_call(
        functools.partial(kernel, sizes),
        out_shape=(out, out),
        in_specs=[hbm] * 5,
        out_specs=(vmem, vmem),
        scratch_shapes=[
            pltpu.SMEM((nights,), jnp.int32),
            pltpu.SMEM((nights,), jnp.int32),
            pltpu.VMEM((nights, bls, block), jnp.int32),
            pltpu.VMEM(visibility.shape, bf16),
            pltpu.VMEM((nights, block * bls, LANES), f32),
            pltpu.VMEM((tiles, lst_n, nights, block, LANES), bf16),
            pltpu.VMEM((tiles, lst_n, nights, block, LANES), bf16),
            pltpu.VMEM((bls, nights, LANES), f32),
            pltpu.VMEM((lst_n, nights, LANES), f32),
            pltpu.VMEM((nights, bins + block, LANES), f32),
            pltpu.VMEM((nights, bins + block, LANES), f32),
            pltpu.VMEM((nights, bins, LANES), f32),
            pltpu.VMEM((bins, LANES), f32),
            pltpu.VMEM((bins, LANES), f32),
            pltpu.VMEM((bl_n, 2, rows // 2, bins), bf16),
            pltpu.VMEM((bins, LANES), bf16),
            pltpu.VMEM((tiles, lst_n, 2, block, LANES), bf16),
            pltpu.VMEM((tiles, lst_n, 2, block, LANES), bf16),
            dma,
            dma((3,)),
            dma((tiles,)),
            dma((tiles,)),
            dma((2,)),
            dma((2,)),
            dma((2,)),
            dma((tiles,)),
            dma((tiles,)),
        ],
        compiler_params=pltpu.CompilerParams(
            collective_id=0, has_side_effects=True, vmem_limit_bytes=48 * 2**20
        ),
        cost_estimate=pl.CostEstimate(
            flops=2 * bins * bins * tiles * LANES, bytes_accessed=8 * 2**20, transcendentals=0
        ),
    )(
        *[
            pltpu.with_memory_space_constraint(x, pltpu.HBM)
            for x in (
                start_bin,
                coverage,
                jnp.swapaxes(clip_flags, 1, 2),
                visibility,
                fringe_filter,
            )
        ]
    )


def solution(mesh):
    placed = (P(None, "lst", "bl", None), P(), P(), P(None, "lst", "bl"), P("bl", None))
    return jax.shard_map(
        shards,
        mesh=mesh,
        in_specs=placed,
        out_specs=(P("lst", "bl", None), P("lst", "bl", None)),
        check_vma=False,
    )
```

```python
import functools

import jax
import jax.numpy as jnp
from jax import lax
from jax.experimental import pallas as pl
from jax.experimental.pallas import tpu as pltpu
from jax.sharding import PartitionSpec as P

LANES = 128


def total_wait(ref, sem):
    pltpu.make_async_copy(ref, ref, sem).wait()


def kernel(
    sizes,
    start_hbm,
    cover_hbm,
    flags_hbm,
    vis_hbm,
    filt_hbm,
    out_f,
    out_s,
    start_ref,
    cover_ref,
    flags_ref,
    vis,
    stage,
    send_in,
    recv_in,
    w_send,
    w_recv,
    rows,
    w_rows,
    w_al,
    inv_mean,
    inv_var,
    filt,
    means,
    send_out,
    recv_out,
    plane_sem,
    vis_sems,
    small_sems,
    in_send,
    in_recv,
    w_sems,
    f_own,
    f_up_send,
    f_up,
    f_down_send,
    f_down,
    f_swap,
    out_send,
    out_recv,
):
    nights, block, bls, lst_n, bl_n, tiles = sizes
    groups = lst_n // bls
    bins = block * lst_n
    wide = groups * LANES
    me = lax.axis_index("lst")
    zed = lax.axis_index("bl")
    my_b, my_g = me // groups, lax.rem(me, groups)
    core = lax.rem(me, 2)
    partner = me + 1 - 2 * core
    partner_g = my_g + 1 - 2 * core
    half = filt.shape[2]
    up, down = lax.rem(zed + 1, bl_n), lax.rem(zed + bl_n - 1, bl_n)
    up_hops, down_hops = bl_n // 2, (bl_n - 1) // 2

    small = [
        pltpu.make_async_copy(src, dst, small_sems.at[i])
        for i, (src, dst) in enumerate(
            ((start_hbm, start_ref), (cover_hbm, cover_ref), (flags_hbm, flags_ref))
        )
    ]
    loads = [
        pltpu.make_async_copy(
            vis_hbm.at[:, :, :, pl.ds(tile * wide, wide)], vis.at[tile], vis_sems.at[tile]
        )
        for tile in range(tiles)
    ]
    loads[0].start()

    barrier = pltpu.get_barrier_semaphore()
    greeted = 0
    for i in (2, 1, 3):
        for g in (my_g, partner_g):
            q = lax.rem(my_b + i, bls) * groups + g
            pl.semaphore_signal(barrier, 1, device_id={"lst": q})
            greeted += 1
    for i in (4, 5, 3, 2, 6, 1, 7):
        q = my_b * groups + lax.rem(my_g + i, groups)
        pl.semaphore_signal(barrier, 1, device_id={"lst": q})
        greeted += 1

    if bl_n > 1:
        pl.semaphore_signal(barrier, 1, device_id={"bl": down})
        greeted += 1

        @pl.when(up > 0)
        def _():
            pl.semaphore_signal(barrier, 1, device_id={"bl": up})

    for copy in small:
        copy.start()
    own_half = pltpu.make_async_copy(
        filt_hbm.at[pl.ds(pl.multiple_of(core * half, half), half)], filt.at[zed, core], f_own
    )
    own_half.start()
    for load in loads[1:]:
        load.start()

    def regroup(tile, group):
        lanes = pl.ds(pl.multiple_of(group * LANES, LANES), LANES)
        for n in range(nights):
            for t in range(block):
                stage[n, t * bls : (t + 1) * bls, :] = vis[tile, n, t, :, lanes].astype(
                    jnp.float32
                )
            for b in range(bls):
                piece = stage[n, pl.ds(b, block, stride=bls), :]
                send_in[tile, b * groups + group, n] = piece.astype(jnp.bfloat16)

    def order(step):
        far = (step + 1) // 2
        return lax.rem(my_g + jnp.where(lax.rem(step, 2) == 1, far, groups - far), groups)

    def send_one(tile, b, group):
        q = b * groups + group
        pltpu.make_async_remote_copy(
            send_in.at[tile, q],
            recv_in.at[tile, me],
            in_send.at[tile],
            in_recv.at[tile],
            device_id={"lst": q},
        ).start()

    def send_row(tile, group):
        @pl.when(group != my_g)
        def _():
            send_one(tile, my_b, group)

        @pl.when(group == my_g)
        def _():
            pltpu.make_async_copy(
                send_in.at[tile, me], recv_in.at[tile, me], in_recv.at[tile]
            ).start()

    def send_rest(tile, group):
        for i in (1, 3, 2):
            send_one(tile, lax.rem(my_b + i, bls), group)

    def send_half(source, to, send_sem, recv_sem):
        return pltpu.make_async_remote_copy(
            filt.at[source, core],
            filt.at[source, core],
            send_sem,
            recv_sem,
            device_id={"bl": to},
        )

    def give_half(source):
        pltpu.make_async_remote_copy(
            filt.at[source, core],
            filt.at[source, core],
            f_swap.at[0],
            f_swap.at[1],
            device_id={"lst": partner},
        ).start()

    def pass_half(hops):
        if hops > up_hops:
            return
        source = lax.rem(zed + bl_n - hops, bl_n)
        total_wait(filt.at[0, core], f_up.at[hops - 1])
        if hops < up_hops:
            send_half(source, up, f_up_send.at[hops], f_up.at[hops]).start()
        give_half(source)
        if hops == 1 and down_hops:

            @pl.when(zed == 0)
            def _():
                send_half(zed, down, f_down_send.at[0], f_down.at[0]).start()

        if hops <= down_hops:
            source = lax.rem(zed + hops, bl_n)
            total_wait(filt.at[0, core], f_down.at[hops - 1])
            if hops < down_hops:
                send_half(source, down, f_down_send.at[hops], f_down.at[hops]).start()
            give_half(source)

    loads[0].wait()
    regroup(0, order(0))
    own_half.wait()
    pl.semaphore_wait(barrier, greeted + (jnp.where(zed > 0, 1, 0) if bl_n > 1 else 0))

    for i in (4, 2, 6):
        q = my_b * groups + lax.rem(my_g + i, groups)
        pl.semaphore_signal(plane_sem, 1, device_id={"lst": q})

    if up_hops:
        send_half(zed, up, f_up_send.at[0], f_up.at[0]).start()
    if down_hops:

        @pl.when(zed > 0)
        def _():
            send_half(zed, down, f_down_send.at[0], f_down.at[0]).start()

    give_half(zed)

    def send_near(step, _):
        group = order(step)

        @pl.when(step > 0)
        def _():
            regroup(0, group)

        send_row(0, group)

        @pl.when(jnp.logical_or(group == my_g, group == partner_g))
        def _():
            send_rest(0, group)

        return 0

    lax.fori_loop(0, groups, send_near, 0)

    pl.semaphore_wait(plane_sem, 3)

    def send_far(step, _):
        group = order(step)

        @pl.when(jnp.logical_and(group != my_g, group != partner_g))
        def _():
            send_rest(0, group)

        return 0

    lax.fori_loop(0, groups, send_far, 0)

    pass_half(1)

    for copy in small:
        copy.wait()
    lane = lax.broadcasted_iota(jnp.int32, (1, block), 1) + me * block
    for b in range(bls):
        parts = []
        for n in range(nights):
            good = jnp.logical_and(lane < cover_ref[n], flags_ref[n, b : b + 1, :] == 0)
            parts.append(jnp.where(good, 1.0, 0.0).astype(jnp.float32))
        w_send[b] = jnp.concatenate(parts, axis=1)

    def send_weights(i, _):
        q = lax.rem(me + i, lst_n)
        pltpu.make_async_remote_copy(
            w_send.at[q // groups], w_recv.at[me], w_sems.at[0], w_sems.at[1], device_id={"lst": q}
        ).start()
        return 0

    lax.fori_loop(1, lst_n, send_weights, 0)
    pltpu.make_async_copy(w_send.at[my_b], w_recv.at[me], w_sems.at[1]).start()

    for tile in range(1, tiles):
        loads[tile].wait()

        def send_step(step, _):
            group = order(step)
            regroup(tile, group)
            send_row(tile, group)
            send_rest(tile, group)
            return 0

        lax.fori_loop(0, groups, send_step, 0)
        pass_half(1 + tile)

    total_wait(w_recv, w_sems.at[1])
    shape = (block, LANES)
    below_diagonal = lax.broadcasted_iota(jnp.int32, shape, 1) - lax.broadcasted_iota(
        jnp.int32, shape, 0
    )

    def spread_weights(src, _):
        row = jnp.broadcast_to(w_recv[src], shape)
        at = pl.ds(pl.multiple_of(src * block, block), block)
        for n in range(nights):
            own = jnp.where(below_diagonal == n * block, row, 0.0)
            w_rows[n, at, :] = jnp.broadcast_to(jnp.sum(own, axis=1, keepdims=True), shape)
        return 0

    lax.fori_loop(0, lst_n, spread_weights, 0)
    for hops in range(1 + tiles, up_hops + 1):
        pass_half(hops)
    for n in range(nights):
        w_rows[n, bins : bins + block, :] = w_rows[n, 0:block, :]

    def first_row(n, k):
        return lax.rem(k * block + bins - start_ref[n], bins)

    def align_weights(k, _):
        at = pl.ds(pl.multiple_of(k * block, block), block)
        count = jnp.zeros(shape, jnp.float32)
        for n in range(nights):
            w = w_rows[n, pl.ds(first_row(n, k), block), :]
            w_al[n, at, :] = w
            count = count + w
        inv_mean[at, :] = 1.0 / jnp.maximum(count, 1.0)
        inv_var[at, :] = 1.0 / jnp.maximum(count - 1.0, 1.0)
        return 0

    lax.fori_loop(0, lst_n, align_weights, 0)

    def bin_tile(tile):
        total_wait(recv_in.at[tile], in_recv.at[tile])

        def widen(src, _):
            at = pl.ds(pl.multiple_of(src * block, block), block)
            for n in range(nights):
                rows[n, at, :] = recv_in[tile, src, n].astype(jnp.float32)
            return 0

        lax.fori_loop(0, lst_n, widen, 0)
        for n in range(nights):
            rows[n, bins : bins + block, :] = rows[n, 0:block, :]

        def moments(k, _):
            at = pl.ds(pl.multiple_of(k * block, block), block)
            x = [rows[n, pl.ds(first_row(n, k), block), :] for n in range(nights)]
            w = [w_al[n, at, :] for n in range(nights)]
            total = x[0] * w[0]
            for n in range(1, nights):
                total = total + x[n] * w[n]
            mean = total * inv_mean[at, :]
            square = jnp.zeros(shape, jnp.float32)
            for n in range(nights):
                off = x[n] - mean
                square = square + w[n] * (off * off)
            means[at, tile * LANES : (tile + 1) * LANES] = mean.astype(jnp.bfloat16)
            send_out[tile, k, 1] = (square * inv_var[at, :]).astype(jnp.bfloat16)
            return 0

        lax.fori_loop(0, lst_n, moments, 0)

    def filter_tiles(first, last):
        def apply_filter(z, _):
            product = jnp.dot(
                filt[z].reshape(2 * half, bins),
                means[:, first * LANES : last * LANES],
                preferred_element_type=jnp.float32,
            ).astype(jnp.bfloat16)
            per = 2 * half // block
            for tile in range(first, last):
                lanes = slice((tile - first) * LANES, (tile - first + 1) * LANES)
                for r in range(per):
                    send_out[tile, z * per + r, 0] = product[r * block : (r + 1) * block, lanes]
            return 0

        lax.fori_loop(0, bl_n, apply_filter, 0)
        for tile in range(first, last):

            def send_back(i, _):
                q = lax.rem(me + i, lst_n)
                pltpu.make_async_remote_copy(
                    send_out.at[tile, q],
                    recv_out.at[tile, me],
                    out_send.at[tile],
                    out_recv.at[tile],
                    device_id={"lst": q},
                ).start()
                return 0

            lax.fori_loop(1, lst_n, send_back, 0)
            pltpu.make_async_copy(
                send_out.at[tile, me], recv_out.at[tile, me], out_recv.at[tile]
            ).start()

    for tile in range(tiles - 1):
        bin_tile(tile)
    total_wait(filt.at[:, 1 - core], f_swap.at[1])
    filter_tiles(0, tiles - 1)
    bin_tile(tiles - 1)
    filter_tiles(tiles - 1, tiles)

    def place_tile(tile, _):
        total_wait(recv_out.at[tile], out_recv.at[tile])

        def place(group, _):
            lanes = pl.ds(pl.multiple_of((tile * groups + group) * LANES, LANES), LANES)
            for which, out in ((0, out_f), (1, out_s)):
                for b in range(bls):
                    stage[which, pl.ds(b, block, stride=bls), :] = recv_out[
                        tile, b * groups + group, which
                    ].astype(jnp.float32)
                for t in range(block):
                    out[t, :, lanes] = stage[which, t * bls : (t + 1) * bls, :].astype(
                        jnp.bfloat16
                    )
            return 0

        lax.fori_loop(0, groups, place, 0)
        return 0

    lax.fori_loop(0, tiles, place_tile, 0)

    for tile in range(tiles):
        total_wait(send_in.at[tile, pl.ds(0, lst_n - 1)], in_send.at[tile])
        total_wait(send_out.at[tile, pl.ds(0, lst_n - 1)], out_send.at[tile])
    total_wait(w_recv.at[pl.ds(0, lst_n - 1)], w_sems.at[0])
    total_wait(filt.at[:, 0], f_swap.at[0])

    for hops in range(up_hops):
        total_wait(filt.at[0, 0], f_up_send.at[hops])
    for hops in range(down_hops):
        total_wait(filt.at[0, 0], f_down_send.at[hops])


def shards(visibility, start_bin, coverage, clip_flags, fringe_filter):
    lst_n, bl_n = lax.axis_size("lst"), lax.axis_size("bl")
    nights, block, bls, width = visibility.shape
    rows, bins = fringe_filter.shape
    groups = lst_n // bls
    tiles = width // (groups * LANES)
    sizes = (nights, block, bls, lst_n, bl_n, tiles)
    bf16, f32 = jnp.bfloat16, jnp.float32
    out = jax.ShapeDtypeStruct((block, bls, width), bf16)
    vmem = pl.BlockSpec(memory_space=pltpu.VMEM)
    hbm = pl.BlockSpec(memory_space=pltpu.HBM)
    dma = pltpu.SemaphoreType.DMA
    return pl.pallas_call(
        functools.partial(kernel, sizes),
        out_shape=(out, out),
        in_specs=[hbm] * 5,
        out_specs=(vmem, vmem),
        scratch_shapes=[
            pltpu.SMEM((nights,), jnp.int32),
            pltpu.SMEM((nights,), jnp.int32),
            pltpu.VMEM((nights, bls, block), jnp.int32),
            pltpu.VMEM((tiles, nights, block, bls, groups * LANES), bf16),
            pltpu.VMEM((nights, block * bls, LANES), f32),
            pltpu.VMEM((tiles, lst_n, nights, block, LANES), bf16),
            pltpu.VMEM((tiles, lst_n, nights, block, LANES), bf16),
            pltpu.VMEM((bls, 1, nights * block), f32),
            pltpu.VMEM((lst_n, 1, nights * block), f32),
            pltpu.VMEM((nights, bins + block, LANES), f32),
            pltpu.VMEM((nights, bins + block, LANES), f32),
            pltpu.VMEM((nights, bins, LANES), f32),
            pltpu.VMEM((bins, LANES), f32),
            pltpu.VMEM((bins, LANES), f32),
            pltpu.VMEM((bl_n, 2, rows // 2, bins), bf16),
            pltpu.VMEM((bins, tiles * LANES), bf16),
            pltpu.VMEM((tiles, lst_n, 2, block, LANES), bf16),
            pltpu.VMEM((tiles, lst_n, 2, block, LANES), bf16),
            pltpu.SemaphoreType.REGULAR,
            dma((tiles,)),
            dma((3,)),
            dma((tiles,)),
            dma((tiles,)),
            dma((2,)),
            dma,
            dma((bl_n,)),
            dma((bl_n,)),
            dma((bl_n,)),
            dma((bl_n,)),
            dma((2,)),
            dma((tiles,)),
            dma((tiles,)),
        ],
        compiler_params=pltpu.CompilerParams(
            collective_id=0, has_side_effects=True, vmem_limit_bytes=48 * 2**20
        ),
        cost_estimate=pl.CostEstimate(
            flops=2 * bins * bins * tiles * LANES, bytes_accessed=8 * 2**20, transcendentals=0
        ),
    )(
        *[
            pltpu.with_memory_space_constraint(x, pltpu.HBM)
            for x in (
                start_bin,
                coverage,
                jnp.swapaxes(clip_flags, 1, 2),
                visibility,
                fringe_filter,
            )
        ]
    )


def solution(mesh):
    placed = (P(None, "lst", "bl", None), P(), P(), P(None, "lst", "bl"), P("bl", None))
    return jax.shard_map(
        shards,
        mesh=mesh,
        in_specs=placed,
        out_specs=(P("lst", "bl", None), P("lst", "bl", None)),
        check_vma=False,
    )
```

```python
import functools

import jax
import jax.numpy as jnp
from jax import lax
from jax.experimental import pallas as pl
from jax.experimental.pallas import tpu as pltpu
from jax.sharding import PartitionSpec as P

LANES = 128
FAR_TO_NEAR = (
    ((2, 2), (2, 1), (2, 3), (1, 2), (3, 2), (1, 1), (3, 3), (1, 3), (3, 1))
    + ((2, 0), (0, 2), (1, 0), (3, 0), (0, 1), (0, 3))
)


def total_wait(ref, sem):
    pltpu.make_async_copy(ref, ref, sem).wait()


def kernel(
    sizes,
    start_hbm,
    cover_hbm,
    flags_hbm,
    vis_hbm,
    filt_hbm,
    out,
    start_ref,
    cover_ref,
    flags_ref,
    vis,
    stage,
    send_in,
    recv_in,
    w_send,
    w_recv,
    rows,
    w_rows,
    w_al,
    inv_mean,
    inv_var,
    filt,
    means,
    send_out,
    recv_out,
    pair_sem,
    plane_sem,
    vis_sems,
    small_sems,
    in_send,
    in_recv,
    w_sems,
    f_own,
    f_up_send,
    f_up,
    f_down_send,
    f_down,
    f_swap,
    out_send,
    out_recv,
):
    nights, block, bls, lst_n, bl_n, tiles = sizes
    groups = lst_n // bls
    bins = block * lst_n
    wide = groups * LANES
    me = lax.axis_index("lst")
    zed = lax.axis_index("bl")
    my_b, my_g = me // groups, lax.rem(me, groups)
    core = lax.rem(me, 2)
    partner = me + 1 - 2 * core
    partner_g = my_g + 1 - 2 * core
    half = filt.shape[2]
    up, down = lax.rem(zed + 1, bl_n), lax.rem(zed + bl_n - 1, bl_n)
    up_hops, down_hops = bl_n // 2, (bl_n - 1) // 2

    small = [
        pltpu.make_async_copy(src, dst, small_sems.at[i])
        for i, (src, dst) in enumerate(
            ((start_hbm, start_ref), (cover_hbm, cover_ref), (flags_hbm, flags_ref))
        )
    ]
    loads = [
        pltpu.make_async_copy(
            vis_hbm.at[:, :, :, pl.ds(tile * wide, wide)], vis.at[tile], vis_sems.at[tile]
        )
        for tile in range(tiles)
    ]

    barrier = pltpu.get_barrier_semaphore()
    greeted = 7
    for i in (2, 1, 3):
        q = lax.rem(my_b + i, bls) * groups + my_g
        pl.semaphore_signal(barrier, 1, device_id={"lst": q})
    for i in (4, 2, 6):
        q = my_b * groups + lax.rem(my_g + i, groups)
        pl.semaphore_signal(barrier, 1, device_id={"lst": q})
    pl.semaphore_signal(barrier, 1, device_id={"lst": partner})
    if bl_n > 1:
        pl.when(zed < bl_n - 1)(
            lambda: pl.semaphore_signal(barrier, 1, device_id={"bl": zed + 1})
        )
        pl.when(zed == 0)(
            lambda: pl.semaphore_signal(barrier, 1, device_id={"bl": bl_n - 1})
        )

    loads[0].start()
    for copy in small:
        copy.start()
    own_half = pltpu.make_async_copy(
        filt_hbm.at[pl.ds(pl.multiple_of(core * half, half), half)], filt.at[zed, core], f_own
    )
    own_half.start()
    for load in loads[1:]:
        load.start()

    def regroup(tile, group):
        lanes = pl.ds(pl.multiple_of(group * LANES, LANES), LANES)
        for n in range(nights):
            for t in range(block):
                stage[n, t * bls : (t + 1) * bls, :] = vis[tile, n, t, :, lanes].astype(
                    jnp.float32
                )
            for b in range(bls):
                piece = stage[n, pl.ds(b, block, stride=bls), :]
                send_in[tile, b * groups + group, n] = piece.astype(jnp.bfloat16)

    def order(step):
        far = (step + 1) // 2
        return lax.rem(my_g + jnp.where(lax.rem(step, 2) == 1, far, groups - far), groups)

    def send_one(tile, b, group):
        q = b * groups + group
        pltpu.make_async_remote_copy(
            send_in.at[tile, q],
            recv_in.at[tile, me],
            in_send.at[tile],
            in_recv.at[tile],
            device_id={"lst": q},
        ).start()

    def send_row(tile, group):
        @pl.when(group != my_g)
        def _():
            send_one(tile, my_b, group)

        @pl.when(group == my_g)
        def _():
            pltpu.make_async_copy(
                send_in.at[tile, me], recv_in.at[tile, me], in_recv.at[tile]
            ).start()

    def send_rest(tile, group):
        for i in (1, 3, 2):
            send_one(tile, lax.rem(my_b + i, bls), group)

    def send_half(source, to, send_sem, recv_sem):
        return pltpu.make_async_remote_copy(
            filt.at[source, core],
            filt.at[source, core],
            send_sem,
            recv_sem,
            device_id={"bl": to},
        )

    def give_half(source):
        pltpu.make_async_remote_copy(
            filt.at[source, core],
            filt.at[source, core],
            f_swap.at[0],
            f_swap.at[1],
            device_id={"lst": partner},
        ).start()

    def pass_half(hops):
        if hops <= down_hops:
            above = lax.rem(zed + hops, bl_n)
            total_wait(filt.at[0, core], f_down.at[hops - 1])
            if hops == 1:
                pl.when(zed < bl_n - 1)(own_up)

            def on_down():
                send_half(above, down, f_down_send.at[hops], f_down.at[hops]).start()

            if 1 < hops < down_hops:
                on_down()
            elif hops < down_hops:
                pl.when(zed > 0)(on_down)
            give_half(above)
        if hops <= up_hops:
            below = lax.rem(zed + bl_n - hops, bl_n)
            total_wait(filt.at[0, core], f_up.at[hops - 1])
            if hops == 1:
                pl.when(zed == 0)(own_down)
                if hops < down_hops:
                    pl.when(zed == 0)(on_down)
            if hops < up_hops:
                send_half(below, up, f_up_send.at[hops], f_up.at[hops]).start()
            give_half(below)

    loads[0].wait()
    regroup(0, order(0))
    own_half.wait()
    if bl_n > 1:
        greeted += jnp.where(zed > 0, 1, 0) + jnp.where(zed == bl_n - 1, 1, 0)
    pl.semaphore_wait(barrier, greeted)

    pl.semaphore_signal(pair_sem, 1, device_id={"lst": partner})

    def own_up():
        send_half(zed, up, f_up_send.at[0], f_up.at[0]).start()

    def own_down():
        send_half(zed, down, f_down_send.at[0], f_down.at[0]).start()

    if bl_n > 1:
        pl.when(zed == bl_n - 1)(own_up)
        pl.when(zed > 0)(own_down)
    give_half(zed)

    def send_near(step, _):
        group = order(step)

        @pl.when(step > 0)
        def _():
            regroup(0, group)

        @pl.when(jnp.logical_or(lax.rem(group, 2) == core, group == partner_g))
        def _():
            send_row(0, group)

        @pl.when(group == my_g)
        def _():
            send_rest(0, group)

        return 0

    lax.fori_loop(0, groups, send_near, 0)
    pl.semaphore_wait(pair_sem, 1)

    for i in (4, 2, 6):
        q = my_b * groups + lax.rem(my_g + i, groups)
        pl.semaphore_signal(plane_sem, 1, device_id={"lst": q})

    def send_other(step, _):
        group = order(step)

        @pl.when(jnp.logical_and(lax.rem(group, 2) != core, group != partner_g))
        def _():
            send_row(0, group)

        @pl.when(group == partner_g)
        def _():
            send_rest(0, group)

        return 0

    lax.fori_loop(0, groups, send_other, 0)
    pl.semaphore_wait(plane_sem, 3)

    def send_far(step, _):
        group = order(step)

        @pl.when(jnp.logical_and(group != my_g, group != partner_g))
        def _():
            send_rest(0, group)

        return 0

    lax.fori_loop(0, groups, send_far, 0)

    pass_half(1)

    for copy in small:
        copy.wait()
    lane = lax.broadcasted_iota(jnp.int32, (1, block), 1) + me * block
    for b in range(bls):
        parts = []
        for n in range(nights):
            good = jnp.logical_and(lane < cover_ref[n], flags_ref[n, b : b + 1, :] == 0)
            parts.append(jnp.where(good, 1.0, 0.0).astype(jnp.float32))
        w_send[b] = jnp.concatenate(parts, axis=1)

    def send_weights(i, _):
        q = lax.rem(me + i, lst_n)
        pltpu.make_async_remote_copy(
            w_send.at[q // groups], w_recv.at[me], w_sems.at[0], w_sems.at[1], device_id={"lst": q}
        ).start()
        return 0

    lax.fori_loop(1, lst_n, send_weights, 0)
    pltpu.make_async_copy(w_send.at[my_b], w_recv.at[me], w_sems.at[1]).start()

    for tile in range(1, tiles):
        loads[tile].wait()

        def send_step(step, _):
            group = order(step)
            regroup(tile, group)
            send_row(tile, group)
            send_rest(tile, group)
            return 0

        lax.fori_loop(0, groups, send_step, 0)
        pass_half(1 + tile)

    total_wait(w_recv, w_sems.at[1])
    shape = (block, LANES)
    below_diagonal = lax.broadcasted_iota(jnp.int32, shape, 1) - lax.broadcasted_iota(
        jnp.int32, shape, 0
    )

    def spread_weights(src, _):
        row = jnp.broadcast_to(w_recv[src], shape)
        at = pl.ds(pl.multiple_of(src * block, block), block)
        for n in range(nights):
            own = jnp.where(below_diagonal == n * block, row, 0.0)
            w_rows[n, at, :] = jnp.broadcast_to(jnp.sum(own, axis=1, keepdims=True), shape)
        return 0

    lax.fori_loop(0, lst_n, spread_weights, 0)
    for hops in range(1 + tiles, up_hops + 1):
        pass_half(hops)
    for n in range(nights):
        w_rows[n, bins : bins + block, :] = w_rows[n, 0:block, :]

    def first_row(n, k):
        return lax.rem(k * block + bins - start_ref[n], bins)

    def align_weights(k, _):
        at = pl.ds(pl.multiple_of(k * block, block), block)
        count = jnp.zeros(shape, jnp.float32)
        for n in range(nights):
            w = w_rows[n, pl.ds(first_row(n, k), block), :]
            w_al[n, at, :] = w
            count = count + w
        inv_mean[at, :] = 1.0 / jnp.maximum(count, 1.0)
        inv_var[at, :] = 1.0 / jnp.maximum(count - 1.0, 1.0)
        return 0

    lax.fori_loop(0, lst_n, align_weights, 0)

    def arrived(tile):
        total_wait(recv_in.at[tile], in_recv.at[tile])

    def bin_tile(tile):
        def widen(src, _):
            at = pl.ds(pl.multiple_of(src * block, block), block)
            for n in range(nights):
                rows[n, at, :] = recv_in[tile, src, n].astype(jnp.float32)
            return 0

        lax.fori_loop(0, lst_n, widen, 0)
        for n in range(nights):
            rows[n, bins : bins + block, :] = rows[n, 0:block, :]

        def moments(k, _):
            at = pl.ds(pl.multiple_of(k * block, block), block)
            x = [rows[n, pl.ds(first_row(n, k), block), :] for n in range(nights)]
            w = [w_al[n, at, :] for n in range(nights)]
            total = x[0] * w[0]
            for n in range(1, nights):
                total = total + x[n] * w[n]
            mean = total * inv_mean[at, :]
            square = jnp.zeros(shape, jnp.float32)
            for n in range(nights):
                off = x[n] - mean
                square = square + w[n] * (off * off)
            means[at, tile * LANES : (tile + 1) * LANES] = mean.astype(jnp.bfloat16)
            send_out[tile, k, 1] = (square * inv_var[at, :]).astype(jnp.bfloat16)
            return 0

        lax.fori_loop(0, lst_n, moments, 0)

    def filter_tiles(first, last):
        def apply_filter(z, _):
            product = jnp.dot(
                filt[z].reshape(2 * half, bins),
                means[:, first * LANES : last * LANES],
                preferred_element_type=jnp.float32,
            ).astype(jnp.bfloat16)
            per = 2 * half // block
            for tile in range(first, last):
                lanes = slice((tile - first) * LANES, (tile - first + 1) * LANES)
                for r in range(per):
                    send_out[tile, z * per + r, 0] = product[r * block : (r + 1) * block, lanes]
            return 0

        lax.fori_loop(0, bl_n, apply_filter, 0)

    def send_back(tile):
        for db, dx in FAR_TO_NEAR:
            for dc in (0, 1):
                b = lax.rem(my_b + db, bls)
                group = lax.rem(jnp.where(dc == 1, partner_g, my_g) + 2 * dx, groups)
                send_result(tile, b * groups + group)
        send_result(tile, partner)
        pltpu.make_async_copy(
            send_out.at[tile, me], recv_out.at[tile, me], out_recv.at[tile]
        ).start()

    def send_result(tile, q):
        pltpu.make_async_remote_copy(
            send_out.at[tile, q],
            recv_out.at[tile, me],
            out_send.at[tile],
            out_recv.at[tile],
            device_id={"lst": q},
        ).start()

    for tile in range(tiles - 1):
        arrived(tile)
        bin_tile(tile)
    total_wait(filt.at[:, 1 - core], f_swap.at[1])
    filter_tiles(0, tiles - 1)
    for tile in range(tiles - 1):
        send_back(tile)
    arrived(tiles - 1)
    bin_tile(tiles - 1)
    filter_tiles(tiles - 1, tiles)
    send_back(tiles - 1)

    def place_tile(tile, _):
        total_wait(recv_out.at[tile], out_recv.at[tile])

        def place(group, _):
            lanes = pl.ds(pl.multiple_of((tile * groups + group) * LANES, LANES), LANES)
            for which in range(2):
                for b in range(bls):
                    stage[which, pl.ds(b, block, stride=bls), :] = recv_out[
                        tile, b * groups + group, which
                    ].astype(jnp.float32)
                for t in range(block):
                    out[which, t, :, lanes] = stage[which, t * bls : (t + 1) * bls, :].astype(
                        jnp.bfloat16
                    )
            return 0

        lax.fori_loop(0, groups, place, 0)
        return 0

    lax.fori_loop(0, tiles, place_tile, 0)

    for tile in range(tiles):
        total_wait(send_in.at[tile, pl.ds(0, lst_n - 1)], in_send.at[tile])
        total_wait(send_out.at[tile, pl.ds(0, lst_n - 1)], out_send.at[tile])
    total_wait(w_recv.at[pl.ds(0, lst_n - 1)], w_sems.at[0])
    total_wait(filt.at[:, 0], f_swap.at[0])

    for hops in range(up_hops):
        total_wait(filt.at[0, 0], f_up_send.at[hops])
    for hops in range(down_hops):
        total_wait(filt.at[0, 0], f_down_send.at[hops])


def shards(visibility, start_bin, coverage, clip_flags, fringe_filter):
    lst_n, bl_n = lax.axis_size("lst"), lax.axis_size("bl")
    nights, block, bls, width = visibility.shape
    rows, bins = fringe_filter.shape
    groups = lst_n // bls
    tiles = width // (groups * LANES)
    sizes = (nights, block, bls, lst_n, bl_n, tiles)
    bf16, f32 = jnp.bfloat16, jnp.float32
    out = jax.ShapeDtypeStruct((2, block, bls, width), bf16)
    vmem = pl.BlockSpec(memory_space=pltpu.VMEM)
    hbm = pl.BlockSpec(memory_space=pltpu.HBM)
    dma = pltpu.SemaphoreType.DMA
    both = pl.pallas_call(
        functools.partial(kernel, sizes),
        out_shape=out,
        in_specs=[hbm] * 5,
        out_specs=vmem,
        scratch_shapes=[
            pltpu.SMEM((nights,), jnp.int32),
            pltpu.SMEM((nights,), jnp.int32),
            pltpu.VMEM((nights, bls, block), jnp.int32),
            pltpu.VMEM((tiles, nights, block, bls, groups * LANES), bf16),
            pltpu.VMEM((nights, block * bls, LANES), f32),
            pltpu.VMEM((tiles, lst_n, nights, block, LANES), bf16),
            pltpu.VMEM((tiles, lst_n, nights, block, LANES), bf16),
            pltpu.VMEM((bls, 1, nights * block), f32),
            pltpu.VMEM((lst_n, 1, nights * block), f32),
            pltpu.VMEM((nights, bins + block, LANES), f32),
            pltpu.VMEM((nights, bins + block, LANES), f32),
            pltpu.VMEM((nights, bins, LANES), f32),
            pltpu.VMEM((bins, LANES), f32),
            pltpu.VMEM((bins, LANES), f32),
            pltpu.VMEM((bl_n, 2, rows // 2, bins), bf16),
            pltpu.VMEM((bins, tiles * LANES), bf16),
            pltpu.VMEM((tiles, lst_n, 2, block, LANES), bf16),
            pltpu.VMEM((tiles, lst_n, 2, block, LANES), bf16),
            pltpu.SemaphoreType.REGULAR,
            pltpu.SemaphoreType.REGULAR,
            dma((tiles,)),
            dma((3,)),
            dma((tiles,)),
            dma((tiles,)),
            dma((2,)),
            dma,
            dma((bl_n,)),
            dma((bl_n,)),
            dma((bl_n,)),
            dma((bl_n,)),
            dma((2,)),
            dma((tiles,)),
            dma((tiles,)),
        ],
        compiler_params=pltpu.CompilerParams(
            collective_id=0, has_side_effects=True, vmem_limit_bytes=40 * 2**20
        ),
        cost_estimate=pl.CostEstimate(
            flops=2 * bins * bins * tiles * LANES, bytes_accessed=8 * 2**20, transcendentals=0
        ),
    )(
        *[
            pltpu.with_memory_space_constraint(x, pltpu.HBM)
            for x in (
                start_bin,
                coverage,
                jnp.swapaxes(clip_flags, 1, 2),
                visibility,
                fringe_filter,
            )
        ]
    )
    return both[0], both[1]


def solution(mesh):
    placed = (P(None, "lst", "bl", None), P(), P(), P(None, "lst", "bl"), P("bl", None))
    return jax.shard_map(
        shards,
        mesh=mesh,
        in_specs=placed,
        out_specs=(P("lst", "bl", None), P("lst", "bl", None)),
        check_vma=False,
    )
```

```python
import functools

import jax
import jax.numpy as jnp
from jax import lax
from jax.experimental import pallas as pl
from jax.experimental.pallas import tpu as pltpu
from jax.sharding import PartitionSpec as P

LANES = 128
FAR_TO_NEAR = (
    ((2, 2), (2, 1), (2, 3), (1, 2), (3, 2), (1, 1), (3, 3), (1, 3), (3, 1))
    + ((2, 0), (0, 2), (1, 0), (3, 0), (0, 1), (0, 3))
)


def total_wait(ref, sem):
    pltpu.make_async_copy(ref, ref, sem).wait()


def kernel(
    sizes,
    start_hbm,
    cover_hbm,
    flags_hbm,
    vis_hbm,
    filt_hbm,
    out,
    start_ref,
    cover_ref,
    flags_ref,
    vis,
    stage,
    send_in,
    recv_in,
    w_send,
    w_recv,
    rows,
    w_rows,
    w_al,
    inv_mean,
    inv_var,
    filt,
    means,
    send_out,
    recv_out,
    pair_sem,
    plane_sem,
    vis_sems,
    small_sems,
    in_send,
    in_recv,
    w_sems,
    f_own,
    f_up_send,
    f_up,
    f_down_send,
    f_down,
    f_swap,
    out_send,
    out_recv,
):
    nights, block, bls, lst_n, bl_n, tiles = sizes
    groups = lst_n // bls
    bins = block * lst_n
    wide = groups * LANES
    me = lax.axis_index("lst")
    zed = lax.axis_index("bl")
    my_b, my_g = me // groups, lax.rem(me, groups)
    core = lax.rem(me, 2)
    partner = me + 1 - 2 * core
    partner_g = my_g + 1 - 2 * core
    half = filt.shape[2]
    up, down = lax.rem(zed + 1, bl_n), lax.rem(zed + bl_n - 1, bl_n)
    up_hops, down_hops = bl_n // 2, (bl_n - 1) // 2

    small = [
        pltpu.make_async_copy(src, dst, small_sems.at[i])
        for i, (src, dst) in enumerate(
            ((start_hbm, start_ref), (cover_hbm, cover_ref), (flags_hbm, flags_ref))
        )
    ]
    loads = [
        pltpu.make_async_copy(
            vis_hbm.at[:, :, :, pl.ds(tile * wide, wide)], vis.at[tile], vis_sems.at[tile]
        )
        for tile in range(tiles)
    ]

    loads[0].start()
    barrier = pltpu.get_barrier_semaphore()
    greeted = 7
    for i in (2, 1, 3):
        q = lax.rem(my_b + i, bls) * groups + my_g
        pl.semaphore_signal(barrier, 1, device_id={"lst": q})
    for i in (4, 2, 6):
        q = my_b * groups + lax.rem(my_g + i, groups)
        pl.semaphore_signal(barrier, 1, device_id={"lst": q})
    pl.semaphore_signal(barrier, 1, device_id={"lst": partner})
    if bl_n > 1:
        pl.when(zed < bl_n - 1)(
            lambda: pl.semaphore_signal(barrier, 1, device_id={"bl": zed + 1})
        )
        pl.when(zed == 0)(
            lambda: pl.semaphore_signal(barrier, 1, device_id={"bl": bl_n - 1})
        )

    for copy in small:
        copy.start()
    own_half = pltpu.make_async_copy(
        filt_hbm.at[pl.ds(pl.multiple_of(core * half, half), half)], filt.at[zed, core], f_own
    )
    own_half.start()
    for load in loads[1:]:
        load.start()

    def regroup(tile, group):
        lanes = pl.ds(pl.multiple_of(group * LANES, LANES), LANES)
        for n in range(nights):
            for t in range(block):
                stage[n, t * bls : (t + 1) * bls, :] = vis[tile, n, t, :, lanes].astype(
                    jnp.float32
                )
            for b in range(bls):
                piece = stage[n, pl.ds(b, block, stride=bls), :]
                send_in[tile, b * groups + group, n] = piece.astype(jnp.bfloat16)

    def order(step):
        far = (step + 1) // 2
        return lax.rem(my_g + jnp.where(lax.rem(step, 2) == 1, far, groups - far), groups)

    def send_one(tile, b, group):
        q = b * groups + group
        pltpu.make_async_remote_copy(
            send_in.at[tile, q],
            recv_in.at[tile, me],
            in_send.at[tile],
            in_recv.at[tile],
            device_id={"lst": q},
        ).start()

    def send_row(tile, group):
        @pl.when(group != my_g)
        def _():
            send_one(tile, my_b, group)

        @pl.when(group == my_g)
        def _():
            pltpu.make_async_copy(
                send_in.at[tile, me], recv_in.at[tile, me], in_recv.at[tile]
            ).start()

    def send_rest(tile, group):
        for i in (1, 3, 2):
            send_one(tile, lax.rem(my_b + i, bls), group)

    def send_half(source, to, send_sem, recv_sem):
        return pltpu.make_async_remote_copy(
            filt.at[source, core],
            filt.at[source, core],
            send_sem,
            recv_sem,
            device_id={"bl": to},
        )

    def give_half(source):
        pltpu.make_async_remote_copy(
            filt.at[source, core],
            filt.at[source, core],
            f_swap.at[0],
            f_swap.at[1],
            device_id={"lst": partner},
        ).start()

    def pass_half(hops):
        if hops <= down_hops:
            above = lax.rem(zed + hops, bl_n)
            total_wait(filt.at[0, core], f_down.at[hops - 1])
            if hops == 1:
                pl.when(zed < bl_n - 1)(own_up)

            def on_down():
                send_half(above, down, f_down_send.at[hops], f_down.at[hops]).start()

            if 1 < hops < down_hops:
                on_down()
            elif hops < down_hops:
                pl.when(zed > 0)(on_down)
            give_half(above)
        if hops <= up_hops:
            below = lax.rem(zed + bl_n - hops, bl_n)
            total_wait(filt.at[0, core], f_up.at[hops - 1])
            if hops == 1:
                pl.when(zed == 0)(own_down)
                if hops < down_hops:
                    pl.when(zed == 0)(on_down)
            if hops < up_hops:
                send_half(below, up, f_up_send.at[hops], f_up.at[hops]).start()
            give_half(below)

    loads[0].wait()
    regroup(0, order(0))
    own_half.wait()
    if bl_n > 1:
        greeted += jnp.where(zed > 0, 1, 0) + jnp.where(zed == bl_n - 1, 1, 0)
    pl.semaphore_wait(barrier, greeted)

    pl.semaphore_signal(pair_sem, 1, device_id={"lst": partner})

    def own_up():
        send_half(zed, up, f_up_send.at[0], f_up.at[0]).start()

    def own_down():
        send_half(zed, down, f_down_send.at[0], f_down.at[0]).start()

    if bl_n > 1:
        pl.when(zed == bl_n - 1)(own_up)
        pl.when(zed > 0)(own_down)
    give_half(zed)

    def send_near(step, _):
        group = order(step)

        @pl.when(step > 0)
        def _():
            regroup(0, group)

        @pl.when(jnp.logical_or(lax.rem(group, 2) == core, group == partner_g))
        def _():
            send_row(0, group)

        @pl.when(group == my_g)
        def _():
            send_rest(0, group)

        return 0

    lax.fori_loop(0, groups, send_near, 0)
    pl.semaphore_wait(pair_sem, 1)

    for i in (4, 2, 6):
        q = my_b * groups + lax.rem(my_g + i, groups)
        pl.semaphore_signal(plane_sem, 1, device_id={"lst": q})

    def send_other(step, _):
        group = order(step)

        @pl.when(jnp.logical_and(lax.rem(group, 2) != core, group != partner_g))
        def _():
            send_row(0, group)

        @pl.when(group == partner_g)
        def _():
            send_rest(0, group)

        return 0

    lax.fori_loop(0, groups, send_other, 0)
    pl.semaphore_wait(plane_sem, 3)

    def send_far(step, _):
        group = order(step)

        @pl.when(jnp.logical_and(group != my_g, group != partner_g))
        def _():
            send_rest(0, group)

        return 0

    lax.fori_loop(0, groups, send_far, 0)

    pass_half(1)

    for copy in small:
        copy.wait()
    lane = lax.broadcasted_iota(jnp.int32, (1, block), 1) + me * block
    for b in range(bls):
        parts = []
        for n in range(nights):
            good = jnp.logical_and(lane < cover_ref[n], flags_ref[n, b : b + 1, :] == 0)
            parts.append(jnp.where(good, 1.0, 0.0).astype(jnp.float32))
        w_send[b] = jnp.concatenate(parts, axis=1)

    def send_weights(i, _):
        q = lax.rem(me + i, lst_n)
        pltpu.make_async_remote_copy(
            w_send.at[q // groups], w_recv.at[me], w_sems.at[0], w_sems.at[1], device_id={"lst": q}
        ).start()
        return 0

    lax.fori_loop(1, lst_n, send_weights, 0)
    pltpu.make_async_copy(w_send.at[my_b], w_recv.at[me], w_sems.at[1]).start()

    for tile in range(1, tiles):
        loads[tile].wait()

        def send_step(step, _):
            group = order(step)
            regroup(tile, group)
            send_row(tile, group)
            send_rest(tile, group)
            return 0

        lax.fori_loop(0, groups, send_step, 0)
        pass_half(1 + tile)

    total_wait(w_recv, w_sems.at[1])
    shape = (block, LANES)
    below_diagonal = lax.broadcasted_iota(jnp.int32, shape, 1) - lax.broadcasted_iota(
        jnp.int32, shape, 0
    )

    def spread_weights(src, _):
        row = jnp.broadcast_to(w_recv[src], shape)
        at = pl.ds(pl.multiple_of(src * block, block), block)
        for n in range(nights):
            own = jnp.where(below_diagonal == n * block, row, 0.0)
            w_rows[n, at, :] = jnp.broadcast_to(jnp.sum(own, axis=1, keepdims=True), shape)
        return 0

    lax.fori_loop(0, lst_n, spread_weights, 0)
    for hops in range(1 + tiles, up_hops + 1):
        pass_half(hops)
    for n in range(nights):
        w_rows[n, bins : bins + block, :] = w_rows[n, 0:block, :]

    def first_row(n, k):
        return lax.rem(k * block + bins - start_ref[n], bins)

    def align_weights(k, _):
        at = pl.ds(pl.multiple_of(k * block, block), block)
        count = jnp.zeros(shape, jnp.float32)
        for n in range(nights):
            w = w_rows[n, pl.ds(first_row(n, k), block), :]
            w_al[n, at, :] = w
            count = count + w
        inv_mean[at, :] = 1.0 / jnp.maximum(count, 1.0)
        inv_var[at, :] = 1.0 / jnp.maximum(count - 1.0, 1.0)
        return 0

    lax.fori_loop(0, lst_n, align_weights, 0)

    def arrived(tile):
        total_wait(recv_in.at[tile], in_recv.at[tile])

    def bin_tile(tile):
        def widen(src, _):
            at = pl.ds(pl.multiple_of(src * block, block), block)
            for n in range(nights):
                rows[n, at, :] = recv_in[tile, src, n].astype(jnp.float32)
            return 0

        lax.fori_loop(0, lst_n, widen, 0)
        for n in range(nights):
            rows[n, bins : bins + block, :] = rows[n, 0:block, :]

        def moments(k, _):
            at = pl.ds(pl.multiple_of(k * block, block), block)
            x = [rows[n, pl.ds(first_row(n, k), block), :] for n in range(nights)]
            w = [w_al[n, at, :] for n in range(nights)]
            total = x[0] * w[0]
            for n in range(1, nights):
                total = total + x[n] * w[n]
            mean = total * inv_mean[at, :]
            square = jnp.zeros(shape, jnp.float32)
            for n in range(nights):
                off = x[n] - mean
                square = square + w[n] * (off * off)
            means[at, tile * LANES : (tile + 1) * LANES] = mean.astype(jnp.bfloat16)
            send_out[tile, k, 1] = (square * inv_var[at, :]).astype(jnp.bfloat16)
            return 0

        lax.fori_loop(0, lst_n, moments, 0)

    def filter_tiles(first, last):
        def apply_filter(z, _):
            product = jnp.dot(
                filt[z].reshape(2 * half, bins),
                means[:, first * LANES : last * LANES],
                preferred_element_type=jnp.float32,
            ).astype(jnp.bfloat16)
            per = 2 * half // block
            for tile in range(first, last):
                lanes = slice((tile - first) * LANES, (tile - first + 1) * LANES)
                for r in range(per):
                    send_out[tile, z * per + r, 0] = product[r * block : (r + 1) * block, lanes]
            return 0

        lax.fori_loop(0, bl_n, apply_filter, 0)

    def send_back(tile):
        for db, dx in FAR_TO_NEAR:
            for dc in (0, 1):
                b = lax.rem(my_b + db, bls)
                group = lax.rem(jnp.where(dc == 1, partner_g, my_g) + 2 * dx, groups)
                send_result(tile, b * groups + group)
        send_result(tile, partner)
        pltpu.make_async_copy(
            send_out.at[tile, me], recv_out.at[tile, me], out_recv.at[tile]
        ).start()

    def send_result(tile, q):
        pltpu.make_async_remote_copy(
            send_out.at[tile, q],
            recv_out.at[tile, me],
            out_send.at[tile],
            out_recv.at[tile],
            device_id={"lst": q},
        ).start()

    for tile in range(tiles - 1):
        arrived(tile)
        bin_tile(tile)
    total_wait(filt.at[:, 1 - core], f_swap.at[1])
    filter_tiles(0, tiles - 1)
    for tile in range(tiles - 1):
        send_back(tile)
    arrived(tiles - 1)
    bin_tile(tiles - 1)
    filter_tiles(tiles - 1, tiles)
    send_back(tiles - 1)

    def place_tile(tile, _):
        total_wait(recv_out.at[tile], out_recv.at[tile])

        def place(pair, _):
            for which in range(2):
                for i in range(2):
                    for b in range(bls):
                        stage[which, pl.ds(i * bls + b, block, stride=2 * bls), :] = recv_out[
                            tile, b * groups + 2 * pair + i, which
                        ].astype(jnp.float32)
                for t in range(block):
                    out[which, t, tile * (groups // 2) + pair] = stage[
                        which, t * 2 * bls : (t + 1) * 2 * bls, :
                    ].astype(jnp.bfloat16)
            return 0

        lax.fori_loop(0, groups // 2, place, 0)
        return 0

    lax.fori_loop(0, tiles, place_tile, 0)

    for tile in range(tiles):
        total_wait(send_in.at[tile, pl.ds(0, lst_n - 1)], in_send.at[tile])
        total_wait(send_out.at[tile, pl.ds(0, lst_n - 1)], out_send.at[tile])
    total_wait(w_recv.at[pl.ds(0, lst_n - 1)], w_sems.at[0])
    total_wait(filt.at[:, 0], f_swap.at[0])

    for hops in range(up_hops):
        total_wait(filt.at[0, 0], f_up_send.at[hops])
    for hops in range(down_hops):
        total_wait(filt.at[0, 0], f_down_send.at[hops])


def shards(visibility, start_bin, coverage, clip_flags, fringe_filter):
    lst_n, bl_n = lax.axis_size("lst"), lax.axis_size("bl")
    nights, block, bls, width = visibility.shape
    rows, bins = fringe_filter.shape
    groups = lst_n // bls
    tiles = width // (groups * LANES)
    sizes = (nights, block, bls, lst_n, bl_n, tiles)
    bf16, f32 = jnp.bfloat16, jnp.float32
    out = jax.ShapeDtypeStruct((2, block, tiles * groups // 2, 2 * bls, LANES), bf16)
    vmem = pl.BlockSpec(memory_space=pltpu.VMEM)
    hbm = pl.BlockSpec(memory_space=pltpu.HBM)
    dma = pltpu.SemaphoreType.DMA
    both = pl.pallas_call(
        functools.partial(kernel, sizes),
        out_shape=out,
        in_specs=[hbm] * 5,
        out_specs=vmem,
        scratch_shapes=[
            pltpu.SMEM((nights,), jnp.int32),
            pltpu.SMEM((nights,), jnp.int32),
            pltpu.VMEM((nights, bls, block), jnp.int32),
            pltpu.VMEM((tiles, nights, block, bls, groups * LANES), bf16),
            pltpu.VMEM((nights, 2 * block * bls, LANES), f32),
            pltpu.VMEM((tiles, lst_n, nights, block, LANES), bf16),
            pltpu.VMEM((tiles, lst_n, nights, block, LANES), bf16),
            pltpu.VMEM((bls, 1, nights * block), f32),
            pltpu.VMEM((lst_n, 1, nights * block), f32),
            pltpu.VMEM((nights, bins + block, LANES), f32),
            pltpu.VMEM((nights, bins + block, LANES), f32),
            pltpu.VMEM((nights, bins, LANES), f32),
            pltpu.VMEM((bins, LANES), f32),
            pltpu.VMEM((bins, LANES), f32),
            pltpu.VMEM((bl_n, 2, rows // 2, bins), bf16),
            pltpu.VMEM((bins, tiles * LANES), bf16),
            pltpu.VMEM((tiles, lst_n, 2, block, LANES), bf16),
            pltpu.VMEM((tiles, lst_n, 2, block, LANES), bf16),
            pltpu.SemaphoreType.REGULAR,
            pltpu.SemaphoreType.REGULAR,
            dma((tiles,)),
            dma((3,)),
            dma((tiles,)),
            dma((tiles,)),
            dma((2,)),
            dma,
            dma((bl_n,)),
            dma((bl_n,)),
            dma((bl_n,)),
            dma((bl_n,)),
            dma((2,)),
            dma((tiles,)),
            dma((tiles,)),
        ],
        compiler_params=pltpu.CompilerParams(
            collective_id=0, has_side_effects=True, vmem_limit_bytes=40 * 2**20
        ),
        cost_estimate=pl.CostEstimate(
            flops=2 * bins * bins * tiles * LANES, bytes_accessed=8 * 2**20, transcendentals=0
        ),
    )(
        *[
            pltpu.with_memory_space_constraint(x, pltpu.HBM)
            for x in (
                start_bin,
                coverage,
                jnp.swapaxes(clip_flags, 1, 2),
                visibility,
                fringe_filter,
            )
        ]
    )

    def unfold(x):
        x = x.reshape(block, tiles * groups, bls, LANES)
        return jnp.swapaxes(x, 1, 2).reshape(block, bls, width)

    return unfold(both[0]), unfold(both[1])


def solution(mesh):
    placed = (P(None, "lst", "bl", None), P(), P(), P(None, "lst", "bl"), P("bl", None))
    return jax.shard_map(
        shards,
        mesh=mesh,
        in_specs=placed,
        out_specs=(P("lst", "bl", None), P("lst", "bl", None)),
        check_vma=False,
    )
```

```python
import functools

import jax
import jax.numpy as jnp
from jax import lax
from jax.experimental import pallas as pl
from jax.experimental.pallas import tpu as pltpu
from jax.sharding import PartitionSpec as P

LANES = 128
FAR_TO_NEAR = (
    ((2, 2), (2, 1), (2, 3), (1, 2), (3, 2), (1, 1), (3, 3), (1, 3), (3, 1))
    + ((2, 0), (0, 2), (1, 0), (3, 0), (0, 1), (0, 3))
)


def total_wait(ref, sem):
    pltpu.make_async_copy(ref, ref, sem).wait()


def kernel(
    sizes,
    start_hbm,
    cover_hbm,
    flags_hbm,
    vis_hbm,
    filt_hbm,
    out,
    start_ref,
    cover_ref,
    flags_ref,
    vis,
    stage,
    send_in,
    recv_in,
    w_send,
    w_recv,
    rows,
    w_rows,
    w_al,
    inv_mean,
    inv_var,
    filt,
    means,
    send_out,
    recv_out,
    pair_sem,
    plane_sem,
    vis_sems,
    small_sems,
    in_send,
    in_recv,
    w_sems,
    f_own,
    f_up_send,
    f_up,
    f_down_send,
    f_down,
    f_swap,
    out_send,
    out_recv,
):
    nights, block, bls, lst_n, bl_n, tiles = sizes
    groups = lst_n // bls
    bins = block * lst_n
    wide = groups * LANES
    me = lax.axis_index("lst")
    zed = lax.axis_index("bl")
    my_b, my_g = me // groups, lax.rem(me, groups)
    core = lax.rem(me, 2)
    partner = me + 1 - 2 * core
    partner_g = my_g + 1 - 2 * core
    half = filt.shape[2]
    up, down = lax.rem(zed + 1, bl_n), lax.rem(zed + bl_n - 1, bl_n)
    up_hops, down_hops = bl_n // 2, (bl_n - 1) // 2

    small = [
        pltpu.make_async_copy(src, dst, small_sems.at[i])
        for i, (src, dst) in enumerate(
            ((start_hbm, start_ref), (cover_hbm, cover_ref), (flags_hbm, flags_ref))
        )
    ]
    loads = [
        pltpu.make_async_copy(
            vis_hbm.at[:, :, :, pl.ds(tile * wide, wide)], vis.at[tile], vis_sems.at[tile]
        )
        for tile in range(tiles)
    ]

    loads[0].start()
    barrier = pltpu.get_barrier_semaphore()
    greeted = 7
    for i in (2, 1, 3):
        q = lax.rem(my_b + i, bls) * groups + my_g
        pl.semaphore_signal(barrier, 1, device_id={"lst": q})
    for i in (4, 2, 6):
        q = my_b * groups + lax.rem(my_g + i, groups)
        pl.semaphore_signal(barrier, 1, device_id={"lst": q})
    pl.semaphore_signal(barrier, 1, device_id={"lst": partner})
    if bl_n > 1:
        pl.when(zed < bl_n - 1)(
            lambda: pl.semaphore_signal(barrier, 1, device_id={"bl": zed + 1})
        )
        pl.when(zed == 0)(
            lambda: pl.semaphore_signal(barrier, 1, device_id={"bl": bl_n - 1})
        )

    for copy in small:
        copy.start()
    own_half = pltpu.make_async_copy(
        filt_hbm.at[pl.ds(pl.multiple_of(core * half, half), half)], filt.at[zed, core], f_own
    )
    own_half.start()

    def regroup(tile, group):
        lanes = pl.ds(pl.multiple_of(group * LANES, LANES), LANES)
        for n in range(nights):
            for t in range(block):
                stage[n, t * bls : (t + 1) * bls, :] = vis[tile, n, t, :, lanes].astype(
                    jnp.float32
                )
            for b in range(bls):
                piece = stage[n, pl.ds(b, block, stride=bls), :]
                send_in[tile, b * groups + group, n] = piece.astype(jnp.bfloat16)

    def order(step):
        far = (step + 1) // 2
        return lax.rem(my_g + jnp.where(lax.rem(step, 2) == 1, far, groups - far), groups)

    def send_one(tile, b, group):
        q = b * groups + group
        pltpu.make_async_remote_copy(
            send_in.at[tile, q],
            recv_in.at[tile, me],
            in_send.at[tile],
            in_recv.at[tile],
            device_id={"lst": q},
        ).start()

    def send_row(tile, group):
        @pl.when(group != my_g)
        def _():
            send_one(tile, my_b, group)

        @pl.when(group == my_g)
        def _():
            pltpu.make_async_copy(
                send_in.at[tile, me], recv_in.at[tile, me], in_recv.at[tile]
            ).start()

    def send_rest(tile, group):
        for i in (1, 3, 2):
            send_one(tile, lax.rem(my_b + i, bls), group)

    def send_half(source, to, send_sem, recv_sem):
        return pltpu.make_async_remote_copy(
            filt.at[source, core],
            filt.at[source, core],
            send_sem,
            recv_sem,
            device_id={"bl": to},
        )

    def give_half(source):
        pltpu.make_async_remote_copy(
            filt.at[source, core],
            filt.at[source, core],
            f_swap.at[0],
            f_swap.at[1],
            device_id={"lst": partner},
        ).start()

    def pass_half(hops):
        if hops <= down_hops:
            above = lax.rem(zed + hops, bl_n)
            total_wait(filt.at[0, core], f_down.at[hops - 1])
            if hops == 1:
                pl.when(zed < bl_n - 1)(own_up)

            def on_down():
                send_half(above, down, f_down_send.at[hops], f_down.at[hops]).start()

            if 1 < hops < down_hops:
                on_down()
            elif hops < down_hops:
                pl.when(zed > 0)(on_down)
            give_half(above)
        if hops <= up_hops:
            below = lax.rem(zed + bl_n - hops, bl_n)
            total_wait(filt.at[0, core], f_up.at[hops - 1])
            if hops == 1:
                pl.when(zed == 0)(own_down)
                if hops < down_hops:
                    pl.when(zed == 0)(on_down)
            if hops < up_hops:
                send_half(below, up, f_up_send.at[hops], f_up.at[hops]).start()
            give_half(below)

    loads[0].wait()
    for load in loads[1:]:
        load.start()
    regroup(0, order(0))
    own_half.wait()
    if bl_n > 1:
        greeted += jnp.where(zed > 0, 1, 0) + jnp.where(zed == bl_n - 1, 1, 0)
    pl.semaphore_wait(barrier, greeted)

    pl.semaphore_signal(pair_sem, 1, device_id={"lst": partner})

    def own_up():
        send_half(zed, up, f_up_send.at[0], f_up.at[0]).start()

    def own_down():
        send_half(zed, down, f_down_send.at[0], f_down.at[0]).start()

    if bl_n > 1:
        pl.when(zed == bl_n - 1)(own_up)
        pl.when(zed > 0)(own_down)
    give_half(zed)

    def send_near(step, _):
        group = order(step)

        @pl.when(step > 0)
        def _():
            regroup(0, group)

        @pl.when(jnp.logical_or(lax.rem(group, 2) == core, group == partner_g))
        def _():
            send_row(0, group)

        @pl.when(group == my_g)
        def _():
            send_rest(0, group)

        return 0

    lax.fori_loop(0, groups, send_near, 0)
    pl.semaphore_wait(pair_sem, 1)

    for i in (4, 2, 6):
        q = my_b * groups + lax.rem(my_g + i, groups)
        pl.semaphore_signal(plane_sem, 1, device_id={"lst": q})

    def send_other(step, _):
        group = order(step)

        @pl.when(jnp.logical_and(lax.rem(group, 2) != core, group != partner_g))
        def _():
            send_row(0, group)

        @pl.when(group == partner_g)
        def _():
            send_rest(0, group)

        return 0

    lax.fori_loop(0, groups, send_other, 0)
    pl.semaphore_wait(plane_sem, 3)

    def send_far(step, _):
        group = order(step)

        @pl.when(jnp.logical_and(group != my_g, group != partner_g))
        def _():
            send_rest(0, group)

        return 0

    lax.fori_loop(0, groups, send_far, 0)

    pass_half(1)

    for copy in small:
        copy.wait()
    lane = lax.broadcasted_iota(jnp.int32, (1, block), 1) + me * block
    for b in range(bls):
        parts = []
        for n in range(nights):
            good = jnp.logical_and(lane < cover_ref[n], flags_ref[n, b : b + 1, :] == 0)
            parts.append(jnp.where(good, 1.0, 0.0).astype(jnp.float32))
        w_send[b] = jnp.concatenate(parts, axis=1)

    def send_weights(i, _):
        q = lax.rem(me + i, lst_n)
        pltpu.make_async_remote_copy(
            w_send.at[q // groups], w_recv.at[me], w_sems.at[0], w_sems.at[1], device_id={"lst": q}
        ).start()
        return 0

    lax.fori_loop(1, lst_n, send_weights, 0)
    pltpu.make_async_copy(w_send.at[my_b], w_recv.at[me], w_sems.at[1]).start()

    for tile in range(1, tiles):
        loads[tile].wait()

        def send_step(step, _):
            group = order(step)
            regroup(tile, group)
            send_row(tile, group)
            send_rest(tile, group)
            return 0

        lax.fori_loop(0, groups, send_step, 0)
        pass_half(1 + tile)

    total_wait(w_recv, w_sems.at[1])
    shape = (block, LANES)
    below_diagonal = lax.broadcasted_iota(jnp.int32, shape, 1) - lax.broadcasted_iota(
        jnp.int32, shape, 0
    )

    def spread_weights(src, _):
        row = jnp.broadcast_to(w_recv[src], shape)
        at = pl.ds(pl.multiple_of(src * block, block), block)
        for n in range(nights):
            own = jnp.where(below_diagonal == n * block, row, 0.0)
            w_rows[n, at, :] = jnp.broadcast_to(jnp.sum(own, axis=1, keepdims=True), shape)
        return 0

    lax.fori_loop(0, lst_n, spread_weights, 0)
    for hops in range(1 + tiles, up_hops + 1):
        pass_half(hops)
    for n in range(nights):
        w_rows[n, bins : bins + block, :] = w_rows[n, 0:block, :]

    def first_row(n, k):
        return lax.rem(k * block + bins - start_ref[n], bins)

    def align_weights(k, _):
        at = pl.ds(pl.multiple_of(k * block, block), block)
        count = jnp.zeros(shape, jnp.float32)
        for n in range(nights):
            w = w_rows[n, pl.ds(first_row(n, k), block), :]
            w_al[n, at, :] = w
            count = count + w
        inv_mean[at, :] = 1.0 / jnp.maximum(count, 1.0)
        inv_var[at, :] = 1.0 / jnp.maximum(count - 1.0, 1.0)
        return 0

    lax.fori_loop(0, lst_n, align_weights, 0)

    def arrived(tile):
        total_wait(recv_in.at[tile], in_recv.at[tile])

    def bin_tile(tile):
        def widen(src, _):
            at = pl.ds(pl.multiple_of(src * block, block), block)
            for n in range(nights):
                rows[n, at, :] = recv_in[tile, src, n].astype(jnp.float32)
            return 0

        lax.fori_loop(0, lst_n, widen, 0)
        for n in range(nights):
            rows[n, bins : bins + block, :] = rows[n, 0:block, :]

        def moments(k, _):
            at = pl.ds(pl.multiple_of(k * block, block), block)
            x = [rows[n, pl.ds(first_row(n, k), block), :] for n in range(nights)]
            w = [w_al[n, at, :] for n in range(nights)]
            total = x[0] * w[0]
            for n in range(1, nights):
                total = total + x[n] * w[n]
            mean = total * inv_mean[at, :]
            square = jnp.zeros(shape, jnp.float32)
            for n in range(nights):
                off = x[n] - mean
                square = square + w[n] * (off * off)
            means[at, tile * LANES : (tile + 1) * LANES] = mean.astype(jnp.bfloat16)
            send_out[tile, k, 1] = (square * inv_var[at, :]).astype(jnp.bfloat16)
            return 0

        lax.fori_loop(0, lst_n, moments, 0)

    def filter_tiles(first, last):
        def apply_filter(z, _):
            product = jnp.dot(
                filt[z].reshape(2 * half, bins),
                means[:, first * LANES : last * LANES],
                preferred_element_type=jnp.float32,
            ).astype(jnp.bfloat16)
            per = 2 * half // block
            for tile in range(first, last):
                lanes = slice((tile - first) * LANES, (tile - first + 1) * LANES)
                for r in range(per):
                    send_out[tile, z * per + r, 0] = product[r * block : (r + 1) * block, lanes]
            return 0

        lax.fori_loop(0, bl_n, apply_filter, 0)

    def send_back(tile):
        for db, dx in FAR_TO_NEAR:
            for dc in (0, 1):
                b = lax.rem(my_b + db, bls)
                group = lax.rem(jnp.where(dc == 1, partner_g, my_g) + 2 * dx, groups)
                send_result(tile, b * groups + group)
        send_result(tile, partner)
        pltpu.make_async_copy(
            send_out.at[tile, me], recv_out.at[tile, me], out_recv.at[tile]
        ).start()

    def send_result(tile, q):
        pltpu.make_async_remote_copy(
            send_out.at[tile, q],
            recv_out.at[tile, me],
            out_send.at[tile],
            out_recv.at[tile],
            device_id={"lst": q},
        ).start()

    for tile in range(tiles - 1):
        arrived(tile)
        bin_tile(tile)
    total_wait(filt.at[:, 1 - core], f_swap.at[1])
    filter_tiles(0, tiles - 1)
    for tile in range(tiles - 1):
        send_back(tile)
    arrived(tiles - 1)
    bin_tile(tiles - 1)
    filter_tiles(tiles - 1, tiles)
    send_back(tiles - 1)

    def place_tile(tile, _):
        total_wait(recv_out.at[tile], out_recv.at[tile])

        def place(half_of_pairs, _):
            for slot in range(4):
                pair, which = 2 * half_of_pairs + slot // 2, slot % 2
                for i in range(2):
                    for b in range(bls):
                        stage[slot, pl.ds(i * bls + b, block, stride=2 * bls), :] = recv_out[
                            tile, b * groups + 2 * pair + i, which
                        ].astype(jnp.float32)
            for slot in range(4):
                pair, which = 2 * half_of_pairs + slot // 2, slot % 2
                for t in range(block):
                    out[which, t, tile * (groups // 2) + pair] = stage[
                        slot, t * 2 * bls : (t + 1) * 2 * bls, :
                    ].astype(jnp.bfloat16)
            return 0

        lax.fori_loop(0, groups // 4, place, 0)
        return 0

    lax.fori_loop(0, tiles, place_tile, 0)

    for tile in range(tiles):
        total_wait(send_in.at[tile, pl.ds(0, lst_n - 1)], in_send.at[tile])
        total_wait(send_out.at[tile, pl.ds(0, lst_n - 1)], out_send.at[tile])
    total_wait(w_recv.at[pl.ds(0, lst_n - 1)], w_sems.at[0])
    total_wait(filt.at[:, 0], f_swap.at[0])

    for hops in range(up_hops):
        total_wait(filt.at[0, 0], f_up_send.at[hops])
    for hops in range(down_hops):
        total_wait(filt.at[0, 0], f_down_send.at[hops])


def shards(visibility, start_bin, coverage, clip_flags, fringe_filter):
    lst_n, bl_n = lax.axis_size("lst"), lax.axis_size("bl")
    nights, block, bls, width = visibility.shape
    rows, bins = fringe_filter.shape
    groups = lst_n // bls
    tiles = width // (groups * LANES)
    sizes = (nights, block, bls, lst_n, bl_n, tiles)
    bf16, f32 = jnp.bfloat16, jnp.float32
    out = jax.ShapeDtypeStruct((2, block, tiles * groups // 2, 2 * bls, LANES), bf16)
    vmem = pl.BlockSpec(memory_space=pltpu.VMEM)
    hbm = pl.BlockSpec(memory_space=pltpu.HBM)
    dma = pltpu.SemaphoreType.DMA
    both = pl.pallas_call(
        functools.partial(kernel, sizes),
        out_shape=out,
        in_specs=[hbm] * 5,
        out_specs=vmem,
        scratch_shapes=[
            pltpu.SMEM((nights,), jnp.int32),
            pltpu.SMEM((nights,), jnp.int32),
            pltpu.VMEM((nights, bls, block), jnp.int32),
            pltpu.VMEM((tiles, nights, block, bls, groups * LANES), bf16),
            pltpu.VMEM((nights, 2 * block * bls, LANES), f32),
            pltpu.VMEM((tiles, lst_n, nights, block, LANES), bf16),
            pltpu.VMEM((tiles, lst_n, nights, block, LANES), bf16),
            pltpu.VMEM((bls, 1, nights * block), f32),
            pltpu.VMEM((lst_n, 1, nights * block), f32),
            pltpu.VMEM((nights, bins + block, LANES), f32),
            pltpu.VMEM((nights, bins + block, LANES), f32),
            pltpu.VMEM((nights, bins, LANES), f32),
            pltpu.VMEM((bins, LANES), f32),
            pltpu.VMEM((bins, LANES), f32),
            pltpu.VMEM((bl_n, 2, rows // 2, bins), bf16),
            pltpu.VMEM((bins, tiles * LANES), bf16),
            pltpu.VMEM((tiles, lst_n, 2, block, LANES), bf16),
            pltpu.VMEM((tiles, lst_n, 2, block, LANES), bf16),
            pltpu.SemaphoreType.REGULAR,
            pltpu.SemaphoreType.REGULAR,
            dma((tiles,)),
            dma((3,)),
            dma((tiles,)),
            dma((tiles,)),
            dma((2,)),
            dma,
            dma((bl_n,)),
            dma((bl_n,)),
            dma((bl_n,)),
            dma((bl_n,)),
            dma((2,)),
            dma((tiles,)),
            dma((tiles,)),
        ],
        compiler_params=pltpu.CompilerParams(
            collective_id=0, has_side_effects=True, vmem_limit_bytes=40 * 2**20
        ),
        cost_estimate=pl.CostEstimate(
            flops=2 * bins * bins * tiles * LANES, bytes_accessed=8 * 2**20, transcendentals=0
        ),
    )(
        *[
            pltpu.with_memory_space_constraint(x, pltpu.HBM)
            for x in (
                start_bin,
                coverage,
                jnp.swapaxes(clip_flags, 1, 2),
                visibility,
                fringe_filter,
            )
        ]
    )

    def unfold(x):
        x = x.reshape(block, tiles * groups, bls, LANES)
        return jnp.swapaxes(x, 1, 2).reshape(block, bls, width)

    return unfold(both[0]), unfold(both[1])


def solution(mesh):
    placed = (P(None, "lst", "bl", None), P(), P(), P(None, "lst", "bl"), P("bl", None))
    return jax.shard_map(
        shards,
        mesh=mesh,
        in_specs=placed,
        out_specs=(P("lst", "bl", None), P("lst", "bl", None)),
        check_vma=False,
    )
```
